512 devices in a mesh: graph: 8 (over z), feat: 64 (over x, y, core).
Axes of the slice: x: 4, y: 8, z: 8, core: 2. Of those that a mesh axis runs over, the one named last changes fastest.
Arguments:
- features: bfloat16 [32768, 512], P('graph', 'feat'), may hold values from -6 to 6
- w_first: bfloat16 [2, 512, 256], P(None, 'feat'), may hold values from -0.25 to 0.25
- w_second: bfloat16 [2, 256, 256], replicated, may hold values from -0.375 to 0.375
- cotangent: bfloat16 [16384, 256], P(('graph', 'feat')), may hold values from -6 to 6
- nbr_first: int32 [16384, 15], P('graph'), may hold values from 0 to 4095
- send_rows: int32 [512, 8, 8], P(('graph', 'feat')), may hold values from -1 to 31, as said below
- nbr_second: int32 [16384, 10], P(('graph', 'feat')), may hold values from 0 to 95, as said below
Outputs:
- layer_out: bfloat16 [16384, 256], P(('graph', 'feat'))
- grad_second: float32 [2, 256, 256], replicated
- grad_first: float32 [2, 512, 256], P(None, 'feat')
The draws below stay inside these ranges and needn't reach their ends.
Inputs may be any that keep to these rules, and one draw needn't show every extreme that they name: `send_rows`: for each device and partition the used slots come first; a device's own partition gets only -1; every used slot of a device to one partition names a different row; for each feat index some partition other than the last receives all 8 slots used from every other partition. `nbr_second`: each entry below 32 names an owned row; every other entry names a used slot received from another partition.
All inputs are finite; a program needn't handle non-finite values.
Results may differ from the reference program's by a relative error of at most 0.0051.
Values may be sent and summed in bfloat16 or wider, within the bound.
A program may use at most 64 MiB of HBM per device.

```python
import jax
import jax.numpy as jnp
from jax import lax

F = 512
HID = 256
FAN1 = 15
FAN2 = 10
OWN = 32
HALO = 8
ROWS_G = 2048
SRC_G = 4096
N_GRAPH = 8
N_FEAT = 64


def halo_counts(key):
    key = jax.random.fold_in(key, 101)
    key_one, key_two, key_hot = jax.random.split(key, 3)
    shape = (N_FEAT, N_GRAPH, N_GRAPH)
    first = jax.random.randint(key_one, shape, 1, HALO + 1)
    second = jax.random.randint(key_two, shape, 1, HALO + 1)
    base = jnp.minimum(first, second)
    hot = jax.random.randint(key_hot, (N_FEAT,), 0, N_GRAPH - 1)
    receiver = jnp.arange(N_GRAPH)
    full = receiver[None, None, :] == hot[:, None, None]
    counts = jnp.where(full, HALO, base)
    sender = jnp.arange(N_GRAPH)[None, :, None]
    return (jnp.where(sender == receiver[None, None, :], 0, counts), hot)


def draw_send_rows(key, part):
    counts, hot = halo_counts(key)
    key = jax.random.fold_in(key, 1)
    key_start, key_stride = jax.random.split(key)
    shape = (N_GRAPH, N_FEAT, N_GRAPH, 1)
    start = jax.random.randint(key_start, shape, 0, OWN)
    graph_ix = jnp.arange(N_GRAPH)[:, None, None, None]
    peer_ix = jnp.arange(N_GRAPH)[None, None, :, None]
    start = jnp.where(peer_ix == (graph_ix + 1) % N_GRAPH, OWN - 1, start)
    stride = 2 * jax.random.randint(key_stride, shape, 0, max(OWN // 2, 1)) + 1
    slots = jnp.arange(HALO)[None, None, None, :]
    rows = (start + slots * stride) % OWN
    used = jnp.transpose(counts, (1, 0, 2))[..., None] > slots
    return jnp.where(used, rows, -1).reshape(N_GRAPH * N_FEAT, N_GRAPH, HALO).astype(jnp.int32)


def draw_nbr_second(key, part):
    counts, hot = halo_counts(key)
    key = jax.random.fold_in(key, 2)
    key_local, key_coin, key_peer, key_slot = jax.random.split(key, 4)
    shape = (N_GRAPH, N_FEAT, OWN, FAN2)
    local = jax.random.randint(key_local, shape, 0, OWN)
    coin = jax.random.randint(key_coin, shape, 0, 2)
    graph_ix = jnp.arange(N_GRAPH)[:, None, None, None]
    feat_ix = jnp.arange(N_FEAT)[None, :, None, None]
    peer = (graph_ix + 1 + jax.random.randint(key_peer, shape, 0, N_GRAPH - 1)) % N_GRAPH
    have = counts[feat_ix, peer, graph_ix]
    slot = jax.random.randint(key_slot, shape, 0, 1 << 20) % have
    far = OWN + peer * HALO + slot
    result = jnp.where(coin == 0, local, far)
    row_ix = jnp.arange(OWN)[None, None, :, None]
    k_ix = jnp.arange(FAN2)[None, None, None, :]
    is_hot = graph_ix == hot[None, :, None, None]
    result = jnp.where(is_hot & (row_ix == 0) & (k_ix == 0), OWN + N_GRAPH * HALO - 1, result)
    result = jnp.where(is_hot & (row_ix == 0) & (k_ix == 1), 0, result)
    return result.reshape(N_GRAPH * N_FEAT * OWN, FAN2).astype(jnp.int32)


def place_ends(values, rng, least, top_value):
    longest = values.shape.index(max(values.shape))
    spots = []
    for shift in (0, 1):
        where = [jax.random.randint(jax.random.fold_in(rng, axis), (), 0, length) for axis, length in enumerate(values.shape)]
        where[longest] = (where[longest] + shift) % values.shape[longest]
        spots.append(tuple(where))
    return values.at[spots[0]].set(least).at[spots[1]].set(top_value)


def levels(rng, dims, shards, low, top_value):
    def one(position, shards_of):
        draws = jax.random.uniform(jax.random.fold_in(jax.random.fold_in(rng, 6), position), (shards_of,), jnp.float32, low / len(shards), top_value / len(shards))
        return jnp.repeat(jnp.exp(draws), dims[position] // shards_of).reshape((-1,) + (1,) * (len(dims) - position - 1))

    gain = one(*shards[0])
    for cut in shards[1:]:
        gain = gain * one(*cut)
    return gain


def bell_draw(key, extent, spread, most, cuts=(), dtype=jnp.bfloat16):
    array = jax.random.normal(key, extent, jnp.float32) * spread
    if len(cuts) > 0:
        array = levels(key, extent, cuts, -0.22, 0.18) * array
    return jnp.clip(array, min=-most, max=most).astype(dtype)


def setup_inputs(seed: int = 0) -> dict:
    key_list = jax.random.split(jax.random.key(seed), 8)
    return {
        "features": bell_draw(key_list[0], (N_GRAPH * SRC_G, F), 1.0, 6.0, ((0, 8), (1, 64))),
        "w_first": bell_draw(key_list[1], (2, F, HID), F ** -0.5, 0.25, ((1, 64),)),
        "w_second": bell_draw(key_list[2], (2, HID, HID), HID ** -0.5, 0.375),
        "cotangent": bell_draw(key_list[3], (N_GRAPH * ROWS_G, HID), 1.0, 6.0, ((0, 512),)),
        "nbr_first": place_ends(jax.random.randint(key_list[4], (N_GRAPH * ROWS_G, FAN1), 0, SRC_G), jax.random.fold_in(key_list[4], 1), 0, SRC_G - 1).astype(jnp.int32),
        "send_rows": draw_send_rows(jax.random.fold_in(key_list[7], 71), 0),
        "nbr_second": draw_nbr_second(jax.random.fold_in(key_list[7], 71), 0),
    }


def silu_grad(value):
    sig = jax.nn.sigmoid(value)
    return sig * (1.0 + value * (1.0 - sig))

def reference(features, w_first, w_second, cotangent, nbr_first, send_rows, nbr_second):
    high = lax.Precision.HIGHEST
    feats = features.reshape(N_GRAPH, SRC_G, F)
    nbrs = nbr_first.reshape(N_GRAPH, ROWS_G, FAN1)

    def first(args):
        source, near = args
        gathered = source[near].astype(jnp.float32)
        mean_one = (lax.optimization_barrier(jnp.sum(gathered, axis=1)) / FAN1).astype(jnp.bfloat16)
        pre = jnp.dot(source[:ROWS_G], w_first[0], preferred_element_type=jnp.float32)
        pre = pre + jnp.dot(mean_one, w_first[1], preferred_element_type=jnp.float32)
        return (pre, mean_one)
    pre_one, mean_one = lax.map(first, (feats, nbrs))
    hidden = jax.nn.silu(pre_one).astype(jnp.bfloat16)
    h_dev = hidden.reshape(N_GRAPH, N_FEAT, OWN, HID)
    sends = send_rows.reshape(N_GRAPH, N_FEAT, N_GRAPH, HALO)
    recv_idx = jnp.transpose(sends, (2, 1, 0, 3))
    peer_ix = jnp.arange(N_GRAPH)[None, None, :, None]
    feat_ix = jnp.arange(N_FEAT)[None, :, None, None]
    halo = h_dev[peer_ix, feat_ix, jnp.maximum(recv_idx, 0)]
    halo = jnp.where((recv_idx >= 0)[..., None], halo, jnp.zeros_like(halo))
    ext = jnp.concatenate([h_dev, halo.reshape(N_GRAPH, N_FEAT, N_GRAPH * HALO, HID)], axis=2)
    width = OWN + N_GRAPH * HALO
    near_two = nbr_second.reshape(N_GRAPH, N_FEAT, OWN, FAN2)
    counts = jnp.zeros((N_GRAPH, N_FEAT, OWN, width), jnp.float32)
    for k in range(FAN2):
        counts = counts + (near_two[..., k, None] == jnp.arange(width)[None, None, None, :]).astype(jnp.float32)
    mean_two = (jnp.einsum('gfij,gfjh->gfih', counts, ext.astype(jnp.float32), precision=high) / FAN2).astype(jnp.bfloat16)
    w_two = w_second.astype(jnp.float32)
    out = jnp.einsum('gfih,ho->gfio', h_dev.astype(jnp.float32), w_two[0], precision=high)
    out = out + jnp.einsum('gfih,ho->gfio', mean_two.astype(jnp.float32), w_two[1], precision=high)
    layer_out = out.astype(jnp.bfloat16).reshape(N_GRAPH * ROWS_G, HID)
    cot = cotangent.reshape(N_GRAPH, N_FEAT, OWN, HID).astype(jnp.float32)
    grad_self = jnp.einsum('gfih,gfio->ho', h_dev.astype(jnp.float32), cot, precision=high)
    grad_near = jnp.einsum('gfih,gfio->ho', mean_two.astype(jnp.float32), cot, precision=high)
    grad_second = jnp.stack([grad_self, grad_near])
    d_self = jnp.einsum('gfio,ho->gfih', cot, w_two[0], precision=high)
    d_mean = jnp.einsum('gfio,ho->gfih', cot, w_two[1], precision=high) / FAN2
    d_ext = jnp.einsum('gfij,gfih->gfjh', counts, d_mean, precision=high)
    halo_grad = d_ext[:, :, OWN:].reshape(N_GRAPH, N_FEAT, N_GRAPH, HALO, HID).astype(jnp.bfloat16)
    back = jnp.transpose(halo_grad, (2, 1, 0, 3, 4)).astype(jnp.float32)
    onehot = (sends[..., None] == jnp.arange(OWN)[None, None, None, None, :]).astype(jnp.float32)
    d_back = jnp.einsum('pfqsr,pfqsh->pfrh', onehot, back, precision=high)
    d_hidden = d_self + d_ext[:, :, :OWN] + d_back
    pre_dev = pre_one.reshape(N_GRAPH, N_FEAT, OWN, HID)
    d_pre = (d_hidden * silu_grad(pre_dev)).astype(jnp.bfloat16).reshape(N_GRAPH, ROWS_G, HID)
    d_pre32 = d_pre.astype(jnp.float32)
    grad_one = jnp.einsum('grf,grh->fh', feats[:, :ROWS_G].astype(jnp.float32), d_pre32, precision=high)
    grad_two = jnp.einsum('grf,grh->fh', mean_one.astype(jnp.float32), d_pre32, precision=high)
    grad_first = jnp.stack([grad_one, grad_two])
    return (layer_out, grad_second, grad_first)
```

```python
import functools

import jax
import jax.numpy as jnp
from jax import lax
from jax.experimental import pallas as pl
from jax.experimental.pallas import tpu as pltpu
from jax.sharding import PartitionSpec as P

HID = 256
FAN1 = 15
FAN2 = 10
OWN = 32
HALO = 8
SRC = 4096
LO = 256
GROUPS = SRC // LO
BF16 = jnp.bfloat16
F32 = jnp.float32
MESH = pl.DeviceIdType.MESH


def select_tree(values, masks):
    for mask in masks:
        values = [
            jnp.where(mask, values[2 * i + 1], values[2 * i]) for i in range(len(values) // 2)
        ]
    return values[0]


def dot(a, b):
    return jnp.dot(a, b, preferred_element_type=F32)


def dot_lhs_t(a, b):
    return lax.dot_general(a, b, (((0,), (0,)), ((), ())), preferred_element_type=F32)


def dot_rhs_t(a, b):
    return lax.dot_general(a, b, (((1,), (1,)), ((), ())), preferred_element_type=F32)


def split(a):
    high = a.astype(BF16)
    return high, (a - high.astype(F32)).astype(BF16)


def kernel(
    n_graph, n_feat,
    feat_ref, w1_ref, w2_ref, cot_ref, near1_ref, send_ref, near2_ref,
    out_ref, g2_ref, g1_ref,
    table, x_own, x_all, w_all, pre_part, pre_in, d_all, hid_own, hid_in,
    v_out, v_in, e_out, e_in, hh_out, hh_in,
    gs_out, gs_in, gz, gz_in, gfin, gsib, dw_out, dw_in, dz, dz_in,
    send_sem, recv_sem,
):
    n_chip = n_feat // 2
    n_row = n_feat // 4
    targets = n_feat * OWN
    tile = min(512, targets)
    per_tile = tile // 128
    shard = HID // n_chip
    g = lax.axis_index("graph")
    f = lax.axis_index("feat")
    row, part = f // 4, f % 4
    chip, core = f // 2, f % 2
    sibling = f + 1 - 2 * core

    def remote(index, src, dst, graph, feat):
        return pltpu.make_async_remote_copy(
            src_ref=src, dst_ref=dst, send_sem=send_sem.at[index], recv_sem=recv_sem.at[index],
            device_id=(graph, feat), device_id_type=MESH,
        )

    def wait_in(index, ref):
        remote(index, ref, ref, g, sibling).wait_recv()

    def wait_out(index, ref):
        remote(index, ref, ref, g, sibling).wait_send()

    def loop(low, high, step):
        def body(i, carry):
            step(i)
            return carry

        lax.fori_loop(low, high, body, 0)

    barrier = pltpu.get_barrier_semaphore()

    def greet(graph, feat):
        pl.semaphore_signal(barrier, inc=1, device_id=(graph, feat), device_id_type=MESH)

    loop(1, n_chip, lambda j: greet(g, 2 * ((chip + j) % n_chip) + core))
    loop(1, n_graph, lambda j: greet((g + j) % n_graph, f))
    greet(g, sibling)
    greet(g, 4 * row + 3 - part)

    width = OWN + n_graph * HALO
    near2 = near2_ref[...]
    slots = lax.broadcasted_iota(jnp.int32, (width, OWN), 0)
    counts_t = jnp.zeros((width, OWN), F32)
    for k in range(FAN2):
        counts_t = counts_t + jnp.where(slots == near2[k : k + 1], 1.0, 0.0)
    counts_t = counts_t.astype(BF16)
    cot = cot_ref[...]
    e_all = dot(counts_t, cot)
    e_out[...] = e_all[OWN:].reshape(n_graph, HALO, HID)

    for s in range(GROUPS):
        table[s * 8 : (s + 1) * 8, :] = feat_ref[:, s * LO : (s + 1) * LO].astype(F32)
    lows = lax.broadcasted_iota(jnp.int32, (LO, tile), 0).astype(F32).astype(BF16)

    def gather(t):
        columns = pl.ds(pl.multiple_of(t * tile, tile), tile)
        near = near1_ref[:, columns]
        groups = table[...].astype(BF16)
        total = jnp.zeros((8, tile), F32)
        for k in range(FAN1):
            index = near[k : k + 1]
            low = jnp.broadcast_to((index % LO).astype(F32), (16, tile)).astype(BF16)
            low = jnp.concatenate([low] * (LO // 16), axis=0)
            picked = dot(groups, jnp.where(lows == low, jnp.ones((), BF16), jnp.zeros((), BF16)))
            high = jnp.broadcast_to(index // LO, (8, tile))
            masks = [(high // (1 << bit)) % 2 != 0 for bit in range(4)]
            total = total + select_tree([picked[s * 8 : (s + 1) * 8] for s in range(GROUPS)], masks)
        both = jnp.concatenate([feat_ref[:, columns].astype(F32), total / FAN1], axis=0).astype(BF16)
        for i in range(per_tile):
            block = t * per_tile + i
            x_own[block] = both[:, i * 128 : (i + 1) * 128]

    def send_x(t):
        for i in range(per_tile):
            block = t * per_tile + i

            @pl.when(block != row)
            def _():
                remote(1, x_own.at[block], x_all.at[(block - row + n_row) % n_row], g, 4 * block + part).start()

    n_tiles = targets // tile
    early = n_tiles // 2
    loop(0, early, gather)
    pl.semaphore_wait(barrier, n_chip - 1 + n_graph - 1 + 2)
    loop(1, n_row, lambda j: remote(0, w1_ref, w_all.at[j], g, 4 * ((row + j) % n_row) + part).start())
    loop(1, n_graph, lambda j: remote(2, e_out.at[(g + j) % n_graph], e_in.at[g], (g + j) % n_graph, f).start())
    loop(0, early, send_x)

    def gather_send(t):
        gather(t)
        send_x(t)

    loop(early, n_tiles, gather_send)
    w_all[0] = w1_ref[...]
    x_all[0] = x_own[row]

    rows = lax.broadcasted_iota(jnp.int32, (OWN, n_graph * HALO), 0)
    pick_t = jnp.where(rows == send_ref[...], 1.0, 0.0).astype(BF16)
    e_in[g] = jnp.zeros((HALO, HID), F32)
    wait_in(2, e_in.at[pl.ds(0, n_graph - 1)])
    back = e_in[...].reshape(n_graph * HALO, HID)
    back_high, back_low = split(back)
    e_total = (e_all[:OWN] + (dot(pick_t, back_high) + dot(pick_t, back_low))) / FAN2
    e_high, e_low = split(e_total)
    first = jnp.broadcast_to(core, (OWN, HID)) == 0
    cot32, e32 = cot.astype(F32), e_high.astype(F32)
    v_own = jnp.where(first, cot32, e32).astype(BF16)
    v_out[...] = jnp.where(first, e32, cot32).astype(BF16)
    remote(3, v_out, v_in, g, sibling).start()
    d_hidden = dot_rhs_t(cot, w2_ref[0]) + (dot_rhs_t(e_high, w2_ref[1]) + dot_rhs_t(e_low, w2_ref[1]))

    wait_in(0, w_all.at[pl.ds(1, n_row - 1)])
    wait_in(1, x_all.at[pl.ds(1, n_row - 1)])
    x = x_all[...].reshape(n_row * 16, 128)
    pre_part[...] = dot_lhs_t(x, w_all[...].reshape(n_row * 16, HID)).reshape(4, OWN, HID)
    for d in (1, 2, 3):
        remote(4, pre_part.at[(part + d) % 4], pre_in.at[d], g, 4 * row + (part + d) % 4).start()
    wait_in(4, pre_in.at[pl.ds(1, 3)])
    pre = (pre_part[part] + pre_in[1]) + (pre_in[2] + pre_in[3])
    sig = 1.0 / (1.0 + jnp.exp(-pre))
    hidden = (pre * sig).astype(BF16)
    hid_own[...] = hidden
    remote(5, hid_own, hid_in, g, sibling).start()
    d_all[part] = (d_hidden * (sig * (1.0 + pre * (1.0 - sig)))).astype(BF16)
    for d in (1, 2, 3):
        remote(6, d_all.at[part], d_all.at[part], g, 4 * row + (part + d) % 4).start()
    hh_out[...] = dot_lhs_t(pick_t, hidden).reshape(n_graph, HALO, HID)
    loop(1, n_graph, lambda j: remote(7, hh_out.at[(g + j) % n_graph], hh_in.at[g], (g + j) % n_graph, f).start())

    wait_in(3, v_in)
    v_pair = jnp.concatenate([v_own, v_in[...]], axis=0)
    wait_in(5, hid_in)
    grad = dot_lhs_t(jnp.concatenate([hidden, hid_in[...]], axis=0), v_pair).reshape(n_chip, shard, HID)
    gs_out[...] = jnp.concatenate([grad[:, :, :128], grad[:, :, 128:]], axis=1).astype(BF16)

    def send_grad(j):
        peer = (chip + j) % n_chip
        remote(8, gs_out.at[peer], gs_in.at[j], g, 2 * peer + core).start()

    loop(1, n_chip, send_grad)

    wait_in(6, d_all.at[pl.ds(0, 3)])
    dw_out[...] = dot(x, d_all[...].reshape(4 * OWN, HID)).reshape(n_row, 16, HID).astype(BF16)
    loop(1, n_row, lambda j: remote(9, dw_out.at[j], dw_in.at[j], g, 4 * ((row - j + n_row) % n_row) + part).start())

    gs_in[0] = gs_out[chip]
    wait_in(8, gs_in.at[pl.ds(1, n_chip - 1)])
    gz[...] = jnp.sum(gs_in[...].astype(F32), axis=0)
    gz_in[g] = gz[...]
    loop(1, n_graph, lambda j: remote(10, gz, gz_in.at[g], (g + j) % n_graph, f).start())

    hh_in[g] = jnp.zeros((HALO, HID), F32)
    wait_in(7, hh_in.at[pl.ds(0, n_graph - 1)])
    ext = jnp.concatenate([hidden.astype(F32), hh_in[...].reshape(n_graph * HALO, HID)], axis=0).astype(BF16)
    mean2 = (dot_lhs_t(counts_t, ext) / FAN2).astype(BF16)
    out_ref[...] = (dot(hidden, w2_ref[0]) + dot(mean2, w2_ref[1])).astype(BF16)

    wait_in(10, gz_in.at[pl.ds(0, n_graph - 1)])
    gfin[chip] = jnp.sum(gz_in[...], axis=0).astype(BF16)
    loop(1, n_chip, lambda j: remote(11, gfin.at[chip], gfin.at[chip], g, 2 * ((chip + j) % n_chip) + core).start())

    dw_in[0] = dw_out[0]
    wait_in(9, dw_in.at[pl.ds(1, n_row - 1)])
    dz[...] = jnp.sum(dw_in[...].astype(F32), axis=0)
    dz_in[g] = dz[...]
    loop(1, n_graph, lambda j: remote(12, dz, dz_in.at[g], (g + j) % n_graph, f).start())
    wait_in(12, dz_in.at[pl.ds(0, n_graph - 1)])
    g1_ref[...] = jnp.sum(dz_in[...], axis=0).reshape(2, 8, HID)

    def unpack(ref, which):
        both = ref[...].astype(F32)
        g2_ref[which, :, 0:128] = both[:, :shard].reshape(HID, 128)
        g2_ref[which, :, 128:256] = both[:, shard:].reshape(HID, 128)

    wait_in(11, gfin.at[pl.ds(0, n_chip - 1)])
    remote(13, gfin, gsib, g, sibling).start()
    unpack(gfin, core)
    wait_in(13, gsib)
    unpack(gsib, 1 - core)

    wait_out(0, w_all.at[pl.ds(1, n_row - 1)])
    wait_out(1, x_all.at[pl.ds(1, n_row - 1)])
    wait_out(2, e_in.at[pl.ds(0, n_graph - 1)])
    wait_out(3, v_in)
    wait_out(4, pre_in.at[pl.ds(1, 3)])
    wait_out(5, hid_in)
    wait_out(6, d_all.at[pl.ds(0, 3)])
    wait_out(7, hh_in.at[pl.ds(0, n_graph - 1)])
    wait_out(8, gs_in.at[pl.ds(1, n_chip - 1)])
    wait_out(9, dw_in.at[pl.ds(1, n_row - 1)])
    wait_out(10, gz_in.at[pl.ds(0, n_graph - 1)])
    wait_out(11, gfin.at[pl.ds(0, n_chip - 1)])
    wait_out(12, dz_in.at[pl.ds(0, n_graph - 1)])
    wait_out(13, gsib)


def solution(mesh):
    n_graph, n_feat = mesh.shape["graph"], mesh.shape["feat"]
    n_chip, n_row = n_feat // 2, n_feat // 4
    pack = 2 * HID // n_chip

    def body(features, w_first, w_second, cotangent, nbr_first, send_rows, nbr_second):
        vmem = pl.BlockSpec(memory_space=pltpu.VMEM)
        return pl.pallas_call(
            functools.partial(kernel, n_graph, n_feat),
            out_shape=(
                jax.ShapeDtypeStruct((OWN, HID), BF16),
                jax.ShapeDtypeStruct((2, HID, HID), F32),
                jax.ShapeDtypeStruct((2, 8, HID), F32),
            ),
            in_specs=[vmem] * 7,
            out_specs=(vmem,) * 3,
            scratch_shapes=[
                pltpu.VMEM((GROUPS * 8, LO), F32),
                pltpu.VMEM((n_row, 16, 128), BF16),
                pltpu.VMEM((n_row, 16, 128), BF16),
                pltpu.VMEM((n_row, 16, HID), BF16),
                pltpu.VMEM((4, OWN, HID), F32),
                pltpu.VMEM((4, OWN, HID), F32),
                pltpu.VMEM((4, OWN, HID), BF16),
                pltpu.VMEM((OWN, HID), BF16),
                pltpu.VMEM((OWN, HID), BF16),
                pltpu.VMEM((OWN, HID), BF16),
                pltpu.VMEM((OWN, HID), BF16),
                pltpu.VMEM((n_graph, HALO, HID), F32),
                pltpu.VMEM((n_graph, HALO, HID), F32),
                pltpu.VMEM((n_graph, HALO, HID), F32),
                pltpu.VMEM((n_graph, HALO, HID), F32),
                pltpu.VMEM((n_chip, pack, 128), BF16),
                pltpu.VMEM((n_chip, pack, 128), BF16),
                pltpu.VMEM((pack, 128), F32),
                pltpu.VMEM((n_graph, pack, 128), F32),
                pltpu.VMEM((n_chip, pack, 128), BF16),
                pltpu.VMEM((n_chip, pack, 128), BF16),
                pltpu.VMEM((n_row, 16, HID), BF16),
                pltpu.VMEM((n_row, 16, HID), BF16),
                pltpu.VMEM((16, HID), F32),
                pltpu.VMEM((n_graph, 16, HID), F32),
                pltpu.SemaphoreType.DMA((14,)),
                pltpu.SemaphoreType.DMA((14,)),
            ],
            compiler_params=pltpu.CompilerParams(
                collective_id=0, has_side_effects=True, vmem_limit_bytes=40 * 1024 * 1024
            ),
        )(
            features.T,
            w_first.reshape(16, HID),
            w_second,
            cotangent,
            nbr_first.T,
            send_rows.reshape(1, n_graph * HALO),
            nbr_second.T,
        )

    in_specs = (
        P("graph", "feat"),
        P(None, "feat", None),
        P(),
        P(("graph", "feat"), None),
        P("graph", None),
        P(("graph", "feat"), None, None),
        P(("graph", "feat"), None),
    )
    out_specs = (P(("graph", "feat"), None), P(), P(None, "feat", None))
    return jax.shard_map(body, mesh=mesh, in_specs=in_specs, out_specs=out_specs, check_vma=False)
```

```python
import functools

import jax
import jax.numpy as jnp
from jax import lax
from jax.experimental import pallas as pl
from jax.experimental.pallas import tpu as pltpu
from jax.sharding import PartitionSpec as P

HID = 256
FAN1 = 15
FAN2 = 10
OWN = 32
HALO = 8
SRC = 4096
N_X = 4
LO = 256
GROUPS = SRC // LO
BF16 = jnp.bfloat16
F32 = jnp.float32
MESH = pl.DeviceIdType.MESH


def select_tree(values, masks):
    for mask in masks:
        values = [
            jnp.where(mask, values[2 * i + 1], values[2 * i]) for i in range(len(values) // 2)
        ]
    return values[0]


def dot(a, b):
    return jnp.dot(a, b, preferred_element_type=F32)


def dot_lhs_t(a, b):
    return lax.dot_general(a, b, (((0,), (0,)), ((), ())), preferred_element_type=F32)


def dot_rhs_t(a, b):
    return lax.dot_general(a, b, (((1,), (1,)), ((), ())), preferred_element_type=F32)


def outward(n, i):
    return n // 2 + (1 - 2 * (i % 2)) * ((i + 1) // 2)


def split(a):
    high = a.astype(BF16)
    return high, (a - high.astype(F32)).astype(BF16)


def kernel(
    n_graph, n_feat,
    feat_hbm, w1_hbm, w2_hbm, cot_hbm, near1_hbm, send_hbm, near2_hbm,
    out_ref, g2_ref, g1_ref,
    feat_ref, near1_ref, w2_ref, cot_ref, send_ref, near2_ref,
    table, x_own, x_all, w_all, pre_part, pre_in, d_all, hid_own, hid_in,
    v_out, v_in, e_out, e_in, hh_out, hh_in,
    gs_out, gs_in, gz, gz_in, gfin, gsib, dw_out, dw_in, dz, dz_in,
    send_sem, recv_sem, load_sem,
):
    n_chip = n_feat // 2
    n_row = n_feat // 4
    n_y = n_chip // N_X
    n_m = n_y // 2
    targets = n_feat * OWN
    tile = targets // 2
    shard = HID // n_chip
    g = lax.axis_index("graph")
    f = lax.axis_index("feat")
    row, part = f // 4, f % 4
    chip, core = f // 2, f % 2
    sibling = f + 1 - 2 * core

    def chip_at(i):
        x = (chip // n_y + outward(N_X, i % N_X)) % N_X
        y = (chip % n_y + outward(n_y, i // N_X)) % n_y
        return x * n_y + y

    def row_at(i, sign):
        x = (row // n_m + sign * outward(N_X, i % N_X) + N_X) % N_X
        m = (row % n_m + sign * outward(n_m, i // N_X) + n_m) % n_m
        return x * n_m + m

    def graph_at(i):
        return (g + outward(n_graph, i)) % n_graph

    def remote(index, src, dst, graph, feat):
        return pltpu.make_async_remote_copy(
            src_ref=src, dst_ref=dst, send_sem=send_sem.at[index], recv_sem=recv_sem.at[index],
            device_id=(graph, feat), device_id_type=MESH,
        )

    def wait_in(index, ref):
        remote(index, ref, ref, g, sibling).wait_recv()

    def wait_out(index, ref):
        remote(index, ref, ref, g, sibling).wait_send()

    def loop(high, step):
        def body(i, carry):
            step(i)
            return carry

        lax.fori_loop(0, high, body, 0)

    loads = [
        pltpu.make_async_copy(src, dst, load_sem.at[i])
        for i, (src, dst) in enumerate((
            (feat_hbm, feat_ref), (near1_hbm, near1_ref), (w1_hbm, w_all.at[n_row - 1]), (cot_hbm, cot_ref),
            (near2_hbm, near2_ref), (send_hbm, send_ref), (w2_hbm, w2_ref),
        ))
    ]
    for load in loads:
        load.start()

    barrier = pltpu.get_barrier_semaphore()

    def greet(graph, feat):
        pl.semaphore_signal(barrier, inc=1, device_id=(graph, feat), device_id_type=MESH)

    loop(n_chip - 1, lambda i: greet(g, 2 * chip_at(i) + core))
    loop(n_graph - 1, lambda i: greet(graph_at(i), f))
    greet(g, 4 * row + 3 - part)
    greet(g, sibling)

    loads[0].wait()
    loads[1].wait()
    for s in range(GROUPS):
        table[s * 8 : (s + 1) * 8, :] = feat_ref[:, s * LO : (s + 1) * LO].astype(F32)
    lows = lax.broadcasted_iota(jnp.int32, (LO, tile), 0).astype(F32).astype(BF16)

    def gather(t):
        columns = pl.ds(pl.multiple_of(t * tile, tile), tile)
        near = near1_ref[:, columns]
        groups = table[...].astype(BF16)
        total = jnp.zeros((8, tile), F32)
        for k in range(FAN1):
            index = near[k : k + 1]
            low = jnp.broadcast_to((index % LO).astype(F32), (16, tile)).astype(BF16)
            low = jnp.concatenate([low] * (LO // 16), axis=0)
            picked = dot(groups, jnp.where(lows == low, jnp.ones((), BF16), jnp.zeros((), BF16)))
            high = jnp.broadcast_to(index // LO, (8, tile))
            masks = [(high // (1 << bit)) % 2 != 0 for bit in range(4)]
            total = total + select_tree([picked[s * 8 : (s + 1) * 8] for s in range(GROUPS)], masks)
        both = jnp.concatenate([feat_ref[:, columns].astype(F32), total / FAN1], axis=0).astype(BF16)
        for i in range(tile // 128):
            x_own[t * (tile // 128) + i] = both[:, i * 128 : (i + 1) * 128]

    def step(t):
        gather(t)

        @pl.when(t == 0)
        def _():
            pl.semaphore_wait(barrier, n_chip - 1 + n_graph - 1 + 2)
            loads[2].wait()
            own = w_all.at[n_row - 1]
            loop(n_row - 1, lambda i: remote(0, own, w_all.at[i], g, 4 * row_at(i, 1) + part).start())

        def send_x(i):
            block = row_at(i, 1)

            @pl.when(block // (n_row // 2) == t)
            def _():
                remote(1, x_own.at[block], x_all.at[i], g, 4 * block + part).start()

        loop(n_row - 1, send_x)

    loop(2, step)
    x_all[n_row - 1] = x_own[row]

    for load in loads[3:]:
        load.wait()
    width = OWN + n_graph * HALO
    near2 = near2_ref[...]
    slots = lax.broadcasted_iota(jnp.int32, (width, OWN), 0)
    counts_t = jnp.zeros((width, OWN), F32)
    for k in range(FAN2):
        counts_t = counts_t + jnp.where(slots == near2[k : k + 1], 1.0, 0.0)
    counts_t = counts_t.astype(BF16)
    cot = cot_ref[...]
    e_all = dot(counts_t, cot)
    e_out[...] = e_all[OWN:].reshape(n_graph, HALO, HID)
    loop(n_graph - 1, lambda i: remote(2, e_out.at[graph_at(i)], e_in.at[g], graph_at(i), f).start())
    rows = lax.broadcasted_iota(jnp.int32, (OWN, n_graph * HALO), 0)
    sent = send_ref[...]
    sent = jnp.concatenate([sent[p : p + 1] for p in range(n_graph)], axis=1)
    pick_t = jnp.where(rows == sent, 1.0, 0.0).astype(BF16)

    wait_in(0, w_all.at[pl.ds(0, n_row - 1)])
    wait_in(1, x_all.at[pl.ds(0, n_row - 1)])
    x = x_all[...].reshape(n_row * 16, 128)
    pre_part[...] = dot_lhs_t(x, w_all[...].reshape(n_row * 16, HID)).reshape(4, OWN, HID)
    for d in (2, 1, 3):
        remote(4, pre_part.at[(part + d) % 4], pre_in.at[d], g, 4 * row + (part + d) % 4).start()

    e_in[g] = jnp.zeros((HALO, HID), F32)
    wait_in(2, e_in.at[pl.ds(0, n_graph - 1)])
    back = e_in[...].reshape(n_graph * HALO, HID)
    back_high, back_low = split(back)
    e_total = (e_all[:OWN] + (dot(pick_t, back_high) + dot(pick_t, back_low))) / FAN2
    e_high, e_low = split(e_total)
    first = jnp.broadcast_to(core, (OWN, HID)) == 0
    cot32, e32 = cot.astype(F32), e_high.astype(F32)
    v_own = jnp.where(first, cot32, e32).astype(BF16)
    v_out[...] = jnp.where(first, e32, cot32).astype(BF16)
    remote(3, v_out, v_in, g, sibling).start()
    d_hidden = dot_rhs_t(cot, w2_ref[0]) + (dot_rhs_t(e_high, w2_ref[1]) + dot_rhs_t(e_low, w2_ref[1]))

    wait_in(4, pre_in.at[pl.ds(1, 3)])
    pre = (pre_part[part] + pre_in[1]) + (pre_in[2] + pre_in[3])
    sig = 1.0 / (1.0 + jnp.exp(-pre))
    hidden = (pre * sig).astype(BF16)
    hid_own[...] = hidden
    remote(5, hid_own, hid_in, g, sibling).start()
    d_all[part] = (d_hidden * (sig * (1.0 + pre * (1.0 - sig)))).astype(BF16)
    for d in (2, 1, 3):
        remote(6, d_all.at[part], d_all.at[part], g, 4 * row + (part + d) % 4).start()

    wait_in(3, v_in)
    v_pair = jnp.concatenate([v_own, v_in[...]], axis=0)
    wait_in(5, hid_in)
    grad = dot_lhs_t(jnp.concatenate([hidden, hid_in[...]], axis=0), v_pair).reshape(n_chip, shard, HID)
    gs_out[...] = jnp.concatenate([grad[:, :, :128], grad[:, :, 128:]], axis=1).astype(BF16)

    def send_grad(i):
        peer = chip_at(i)
        remote(8, gs_out.at[peer], gs_in.at[i], g, 2 * peer + core).start()

    loop(n_chip - 1, send_grad)
    gs_in[n_chip - 1] = gs_out[chip]

    hh_out[...] = dot_lhs_t(pick_t, hidden).reshape(n_graph, HALO, HID)
    loop(n_graph - 1, lambda i: remote(7, hh_out.at[graph_at(i)], hh_in.at[g], graph_at(i), f).start())

    wait_in(6, d_all.at[pl.ds(0, 3)])
    dw_out[...] = dot(x, d_all[...].reshape(4 * OWN, HID)).reshape(n_row, 16, HID).astype(BF16)
    loop(n_row - 1, lambda i: remote(9, dw_out.at[i], dw_in.at[i], g, 4 * row_at(i, -1) + part).start())
    dw_in[n_row - 1] = dw_out[n_row - 1]

    wait_in(8, gs_in.at[pl.ds(0, n_chip - 1)])
    gz[...] = jnp.sum(gs_in[...].astype(F32), axis=0)
    loop(n_graph - 1, lambda i: remote(10, gz, gz_in.at[g], graph_at(i), f).start())
    gz_in[g] = gz[...]

    hh_in[g] = jnp.zeros((HALO, HID), F32)
    wait_in(7, hh_in.at[pl.ds(0, n_graph - 1)])
    ext = jnp.concatenate([hidden.astype(F32), hh_in[...].reshape(n_graph * HALO, HID)], axis=0).astype(BF16)
    mean2 = (dot_lhs_t(counts_t, ext) / FAN2).astype(BF16)
    out_ref[...] = (dot(hidden, w2_ref[0]) + dot(mean2, w2_ref[1])).astype(BF16)

    wait_in(10, gz_in.at[pl.ds(0, n_graph - 1)])
    gfin[chip] = jnp.sum(gz_in[...], axis=0).astype(BF16)
    loop(n_chip - 1, lambda i: remote(11, gfin.at[chip], gfin.at[chip], g, 2 * chip_at(i) + core).start())

    wait_in(9, dw_in.at[pl.ds(0, n_row - 1)])
    dz[...] = jnp.sum(dw_in[...].astype(F32), axis=0)
    dz_in[g] = dz[...]
    loop(n_graph - 1, lambda i: remote(12, dz, dz_in.at[g], graph_at(i), f).start())
    wait_in(12, dz_in.at[pl.ds(0, n_graph - 1)])
    g1_ref[...] = jnp.sum(dz_in[...], axis=0).reshape(2, 8, HID)

    def unpack(ref, which):
        both = ref[...].astype(F32)
        g2_ref[which, :, 0:128] = both[:, :shard].reshape(HID, 128)
        g2_ref[which, :, 128:256] = both[:, shard:].reshape(HID, 128)

    wait_in(11, gfin.at[pl.ds(0, n_chip - 1)])
    remote(13, gfin, gsib, g, sibling).start()
    unpack(gfin, core)
    wait_in(13, gsib)
    unpack(gsib, 1 - core)

    wait_out(0, w_all.at[pl.ds(0, n_row - 1)])
    wait_out(1, x_all.at[pl.ds(0, n_row - 1)])
    wait_out(2, e_in.at[pl.ds(0, n_graph - 1)])
    wait_out(3, v_in)
    wait_out(4, pre_in.at[pl.ds(1, 3)])
    wait_out(5, hid_in)
    wait_out(6, d_all.at[pl.ds(0, 3)])
    wait_out(7, hh_in.at[pl.ds(0, n_graph - 1)])
    wait_out(8, gs_in.at[pl.ds(0, n_chip - 1)])
    wait_out(9, dw_in.at[pl.ds(0, n_row - 1)])
    wait_out(10, gz_in.at[pl.ds(0, n_graph - 1)])
    wait_out(11, gfin.at[pl.ds(0, n_chip - 1)])
    wait_out(12, dz_in.at[pl.ds(0, n_graph - 1)])
    wait_out(13, gsib)


def store_kernel(a_ref, b_ref, c_ref, a_out, b_out, c_out, sem):
    copies = [
        pltpu.make_async_copy(src, dst, sem.at[i])
        for i, (src, dst) in enumerate(((b_ref, b_out), (a_ref, a_out), (c_ref, c_out)))
    ]
    for copy in copies:
        copy.start()
    for copy in copies:
        copy.wait()


def solution(mesh):
    n_graph, n_feat = mesh.shape["graph"], mesh.shape["feat"]
    n_chip, n_row = n_feat // 2, n_feat // 4
    pack = 2 * HID // n_chip

    def body(features, w_first, w_second, cotangent, nbr_first, send_rows, nbr_second):
        vmem = pl.BlockSpec(memory_space=pltpu.VMEM)
        hbm = pl.BlockSpec(memory_space=pltpu.HBM)
        shapes = (
            jax.ShapeDtypeStruct((OWN, HID), BF16),
            jax.ShapeDtypeStruct((2, HID, HID), F32),
            jax.ShapeDtypeStruct((2, 8, HID), F32),
        )
        results = pl.pallas_call(
            functools.partial(kernel, n_graph, n_feat),
            out_shape=shapes,
            in_specs=[hbm] * 7,
            out_specs=(vmem,) * 3,
            scratch_shapes=[
                pltpu.VMEM((8, SRC), BF16),
                pltpu.VMEM((FAN1, n_feat * OWN), jnp.int32),
                pltpu.VMEM((2, HID, HID), BF16),
                pltpu.VMEM((OWN, HID), BF16),
                pltpu.VMEM((n_graph, HALO), jnp.int32),
                pltpu.VMEM((FAN2, OWN), jnp.int32),
                pltpu.VMEM((GROUPS * 8, LO), F32),
                pltpu.VMEM((n_row, 16, 128), BF16),
                pltpu.VMEM((n_row, 16, 128), BF16),
                pltpu.VMEM((n_row, 16, HID), BF16),
                pltpu.VMEM((4, OWN, HID), F32),
                pltpu.VMEM((4, OWN, HID), F32),
                pltpu.VMEM((4, OWN, HID), BF16),
                pltpu.VMEM((OWN, HID), BF16),
                pltpu.VMEM((OWN, HID), BF16),
                pltpu.VMEM((OWN, HID), BF16),
                pltpu.VMEM((OWN, HID), BF16),
                pltpu.VMEM((n_graph, HALO, HID), F32),
                pltpu.VMEM((n_graph, HALO, HID), F32),
                pltpu.VMEM((n_graph, HALO, HID), F32),
                pltpu.VMEM((n_graph, HALO, HID), F32),
                pltpu.VMEM((n_chip, pack, 128), BF16),
                pltpu.VMEM((n_chip, pack, 128), BF16),
                pltpu.VMEM((pack, 128), F32),
                pltpu.VMEM((n_graph, pack, 128), F32),
                pltpu.VMEM((n_chip, pack, 128), BF16),
                pltpu.VMEM((n_chip, pack, 128), BF16),
                pltpu.VMEM((n_row, 16, HID), BF16),
                pltpu.VMEM((n_row, 16, HID), BF16),
                pltpu.VMEM((16, HID), F32),
                pltpu.VMEM((n_graph, 16, HID), F32),
                pltpu.SemaphoreType.DMA((14,)),
                pltpu.SemaphoreType.DMA((14,)),
                pltpu.SemaphoreType.DMA((7,)),
            ],
            compiler_params=pltpu.CompilerParams(
                collective_id=0, has_side_effects=True, vmem_limit_bytes=40 * 1024 * 1024
            ),
        )(
            *(
                pltpu.with_memory_space_constraint(a, pltpu.HBM)
                for a in (
                    features.T,
                    w_first.reshape(16, HID),
                    w_second,
                    cotangent,
                    nbr_first.T,
                    send_rows.reshape(n_graph, HALO),
                    nbr_second.T,
                )
            )
        )
        return pl.pallas_call(
            store_kernel,
            out_shape=shapes,
            in_specs=[vmem] * 3,
            out_specs=(hbm,) * 3,
            scratch_shapes=[pltpu.SemaphoreType.DMA((3,))],
        )(*results)

    in_specs = (
        P("graph", "feat"),
        P(None, "feat", None),
        P(),
        P(("graph", "feat"), None),
        P("graph", None),
        P(("graph", "feat"), None, None),
        P(("graph", "feat"), None),
    )
    out_specs = (P(("graph", "feat"), None), P(), P(None, "feat", None))
    return jax.shard_map(body, mesh=mesh, in_specs=in_specs, out_specs=out_specs, check_vma=False)
```

```python
import functools

import jax
import jax.numpy as jnp
from jax import lax
from jax.experimental import pallas as pl
from jax.experimental.pallas import tpu as pltpu
from jax.sharding import PartitionSpec as P

HID = 256
FAN1 = 15
FAN2 = 10
OWN = 32
HALO = 8
SRC = 4096
N_X = 4
LO = 256
GROUPS = SRC // LO
BF16 = jnp.bfloat16
F32 = jnp.float32
MESH = pl.DeviceIdType.MESH


def select_tree(values, masks):
    for mask in masks:
        values = [
            jnp.where(mask, values[2 * i + 1], values[2 * i]) for i in range(len(values) // 2)
        ]
    return values[0]


def dot(a, b):
    return jnp.dot(a, b, preferred_element_type=F32)


def dot_lhs_t(a, b):
    return lax.dot_general(a, b, (((0,), (0,)), ((), ())), preferred_element_type=F32)


def dot_rhs_t(a, b):
    return lax.dot_general(a, b, (((1,), (1,)), ((), ())), preferred_element_type=F32)


def outward(n, i):
    return n // 2 + (1 - 2 * (i % 2)) * ((i + 1) // 2)


def split(a):
    high = a.astype(BF16)
    return high, (a - high.astype(F32)).astype(BF16)


def kernel(
    n_graph, n_feat,
    feat_hbm, w1_hbm, w2_hbm, cot_hbm, near1_hbm, send_hbm, near2_hbm,
    out_ref, g2_ref, g1_ref,
    feat_ref, near1_ref, w2_ref, cot_ref, send_ref, near2_ref,
    table, x_own, x_all, w_all, pre_part, pre_in, d_all, hid_own, hid_in,
    v_out, v_in, e_out, e_in, hh_out, hh_in,
    gs_out, gs_in, gz, gz_in, gfin, gsib, dw_out, dw_in, dz, dz_in,
    send_sem, recv_sem, load_sem,
):
    n_chip = n_feat // 2
    n_row = n_feat // 4
    n_y = n_chip // N_X
    n_m = n_y // 2
    targets = n_feat * OWN
    tile = targets // 2
    shard = HID // n_chip
    g = lax.axis_index("graph")
    f = lax.axis_index("feat")
    row, part = f // 4, f % 4
    chip, core = f // 2, f % 2
    sibling = f + 1 - 2 * core
    x, y = chip // n_y, chip % n_y
    sheet = x * n_y + (1 - core) * y + core * g

    depth = (1 - core) * y + core * g
    around = (1 - core) * g + core * y
    turn_x = [(x + outward(N_X, i)) % N_X for i in range(N_X)]
    turn_d = [(depth + outward(n_y, i)) % n_y for i in range(n_y)]
    turn_a = [(around + outward(n_y, i)) % n_y for i in range(n_y)]
    turn_m = [(row % n_m + outward(n_m, i)) % n_m for i in range(n_m)]
    back_x = [(x - outward(N_X, i) + N_X) % N_X for i in range(N_X)]
    back_m = [(row % n_m - outward(n_m, i) + n_m) % n_m for i in range(n_m)]
    graphs = [(g + outward(n_graph, i)) % n_graph for i in range(n_graph - 1)]
    sheet_x = [2 * n_y * to + core for to in turn_x]
    sheet_f = [2 * ((1 - core) * to + core * y) for to in turn_d]
    sheet_g = [(1 - core) * g + core * to for to in turn_d]
    sheet_peers = [
        (turn_x[i % N_X] * n_y + turn_d[i // N_X], sheet_g[i // N_X], sheet_x[i % N_X] + sheet_f[i // N_X])
        for i in range(n_chip - 1)
    ]
    ring_peers = [
        ((1 - core) * to + core * g, 2 * (x * n_y + (1 - core) * y + core * to) + core) for to in turn_a[:-1]
    ]
    row_peers = [turn_x[i % N_X] * n_m + turn_m[i // N_X] for i in range(n_row - 1)]
    row_sources = [back_x[i % N_X] * n_m + back_m[i // N_X] for i in range(n_row - 1)]

    def remote(index, src, dst, graph, feat):
        return pltpu.make_async_remote_copy(
            src_ref=src, dst_ref=dst, send_sem=send_sem.at[index], recv_sem=recv_sem.at[index],
            device_id=(graph, feat), device_id_type=MESH,
        )

    def wait_in(index, ref):
        remote(index, ref, ref, g, sibling).wait_recv()

    def wait_out(index, ref):
        remote(index, ref, ref, g, sibling).wait_send()

    loads = [
        pltpu.make_async_copy(src, dst, load_sem.at[i])
        for i, (src, dst) in enumerate((
            (feat_hbm, feat_ref), (near1_hbm, near1_ref), (w1_hbm, w_all.at[n_row - 1]), (cot_hbm, cot_ref),
            (near2_hbm, near2_ref), (send_hbm, send_ref), (w2_hbm, w2_ref),
        ))
    ]
    for load in loads:
        load.start()

    barrier = pltpu.get_barrier_semaphore()

    def greet(graph, feat):
        pl.semaphore_signal(barrier, inc=1, device_id=(graph, feat), device_id_type=MESH)

    for _, graph, feat in sheet_peers:
        greet(graph, feat)
    for graph, feat in ring_peers:
        greet(graph, feat)

    @pl.when(core == 1)
    def _():
        for i in range(n_row - 1):
            if i % N_X != N_X - 1:
                greet(g, 4 * row_peers[i] + part)

    greet(g, 4 * row + 3 - part)
    greet(g, sibling)

    loads[0].wait()
    loads[1].wait()
    for s in range(GROUPS):
        table[s * 8 : (s + 1) * 8, :] = feat_ref[:, s * LO : (s + 1) * LO].astype(F32)
    lows = lax.broadcasted_iota(jnp.int32, (LO, tile), 0).astype(F32).astype(BF16)

    def gather(t):
        columns = pl.ds(pl.multiple_of(t * tile, tile), tile)
        near = near1_ref[:, columns]
        groups = table[...].astype(BF16)
        total = jnp.zeros((8, tile), F32)
        for k in range(FAN1):
            index = near[k : k + 1]
            low = jnp.broadcast_to((index % LO).astype(F32), (16, tile)).astype(BF16)
            low = jnp.concatenate([low] * (LO // 16), axis=0)
            picked = dot(groups, jnp.where(lows == low, jnp.ones((), BF16), jnp.zeros((), BF16)))
            high = jnp.broadcast_to(index // LO, (8, tile))
            masks = [(high // (1 << bit)) % 2 != 0 for bit in range(4)]
            total = total + select_tree([picked[s * 8 : (s + 1) * 8] for s in range(GROUPS)], masks)
        both = jnp.concatenate([feat_ref[:, columns].astype(F32), total / FAN1], axis=0).astype(BF16)
        for i in range(tile // 128):
            x_own[t * (tile // 128) + i] = both[:, i * 128 : (i + 1) * 128]

    def step(t, carry):
        gather(t)

        @pl.when(t == 0)
        def _():
            pl.semaphore_wait(barrier, n_chip - 1 + n_graph - 1 + 2 + core * (n_row - n_row // N_X))
            loads[2].wait()
            own = w_all.at[n_row - 1]
            for i, peer in enumerate(row_peers):
                remote(0, own, w_all.at[i], g, 4 * peer + part).start()

        for i, block in enumerate(row_peers):

            @pl.when(block // (n_row // 2) == t)
            def _(i=i, block=block):
                remote(1, x_own.at[block], x_all.at[i], g, 4 * block + part).start()

        return carry

    lax.fori_loop(0, 2, step, 0)
    x_all[n_row - 1] = x_own[row]

    for load in loads[3:]:
        load.wait()
    width = OWN + n_graph * HALO
    near2 = near2_ref[...]
    slots = lax.broadcasted_iota(jnp.int32, (width, OWN), 0)
    counts_t = jnp.zeros((width, OWN), F32)
    for k in range(FAN2):
        counts_t = counts_t + jnp.where(slots == near2[k : k + 1], 1.0, 0.0)
    counts_t = counts_t.astype(BF16)
    cot = cot_ref[...]
    e_all = dot(counts_t, cot)
    e_out[...] = e_all[OWN:].reshape(n_graph, HALO, HID)
    for peer in graphs:
        remote(2, e_out.at[peer], e_in.at[g], peer, f).start()
    rows = lax.broadcasted_iota(jnp.int32, (OWN, n_graph * HALO), 0)
    sent = send_ref[...]
    sent = jnp.concatenate([sent[p : p + 1] for p in range(n_graph)], axis=1)
    pick_t = jnp.where(rows == sent, 1.0, 0.0).astype(BF16)

    wait_in(0, w_all.at[pl.ds(0, n_row - 1)])
    wait_in(1, x_all.at[pl.ds(0, n_row - 1)])
    inputs = x_all[...].reshape(n_row * 16, 128)
    pre_part[...] = dot_lhs_t(inputs, w_all[...].reshape(n_row * 16, HID)).reshape(4, OWN, HID)
    for d in (2, 1, 3):
        remote(4, pre_part.at[(part + d) % 4], pre_in.at[d], g, 4 * row + (part + d) % 4).start()

    e_in[g] = jnp.zeros((HALO, HID), F32)
    wait_in(2, e_in.at[pl.ds(0, n_graph - 1)])
    back = e_in[...].reshape(n_graph * HALO, HID)
    back_high, back_low = split(back)
    e_total = (e_all[:OWN] + (dot(pick_t, back_high) + dot(pick_t, back_low))) / FAN2
    e_high, e_low = split(e_total)
    first = jnp.broadcast_to(core, (OWN, HID)) == 0
    cot32, e32 = cot.astype(F32), e_high.astype(F32)
    v_own = jnp.where(first, cot32, e32).astype(BF16)
    v_out[...] = jnp.where(first, e32, cot32).astype(BF16)
    remote(3, v_out, v_in, g, sibling).start()
    d_hidden = dot_rhs_t(cot, w2_ref[0]) + (dot_rhs_t(e_high, w2_ref[1]) + dot_rhs_t(e_low, w2_ref[1]))

    wait_in(4, pre_in.at[pl.ds(1, 3)])
    pre = (pre_part[part] + pre_in[1]) + (pre_in[2] + pre_in[3])
    sig = 1.0 / (1.0 + jnp.exp(-pre))
    hidden = (pre * sig).astype(BF16)
    hid_own[...] = hidden
    remote(5, hid_own, hid_in, g, sibling).start()
    d_all[part] = (d_hidden * (sig * (1.0 + pre * (1.0 - sig)))).astype(BF16)
    for d in (2, 1, 3):
        remote(6, d_all.at[part], d_all.at[part], g, 4 * row + (part + d) % 4).start()

    wait_in(3, v_in)
    v_pair = jnp.concatenate([v_own, v_in[...]], axis=0)
    wait_in(5, hid_in)
    grad = dot_lhs_t(jnp.concatenate([hidden, hid_in[...]], axis=0), v_pair).reshape(n_chip, shard, HID)
    gs_out[...] = jnp.concatenate([grad[:, :, :128], grad[:, :, 128:]], axis=1).astype(BF16)

    for i, (peer, graph, feat) in enumerate(sheet_peers):
        remote(8, gs_out.at[peer], gs_in.at[i], graph, feat).start()
    gs_in[n_chip - 1] = gs_out[sheet]

    hh_out[...] = dot_lhs_t(pick_t, hidden).reshape(n_graph, HALO, HID)
    for peer in graphs:
        remote(7, hh_out.at[peer], hh_in.at[g], peer, f).start()

    wait_in(6, d_all.at[pl.ds(0, 3)])
    dw_out[...] = dot(inputs, d_all[...].reshape(4 * OWN, HID)).reshape(n_row, 16, HID).astype(BF16)
    for i, peer in enumerate(row_sources):
        remote(9, dw_out.at[i], dw_in.at[i], g, 4 * peer + part).start()
    dw_in[n_row - 1] = dw_out[n_row - 1]

    wait_in(8, gs_in.at[pl.ds(0, n_chip - 1)])
    gz[...] = jnp.sum(gs_in[...].astype(F32), axis=0)
    for graph, feat in ring_peers:
        remote(10, gz, gz_in.at[around], graph, feat).start()
    gz_in[around] = gz[...]

    hh_in[g] = jnp.zeros((HALO, HID), F32)
    wait_in(7, hh_in.at[pl.ds(0, n_graph - 1)])
    ext = jnp.concatenate([hidden.astype(F32), hh_in[...].reshape(n_graph * HALO, HID)], axis=0).astype(BF16)
    mean2 = (dot_lhs_t(counts_t, ext) / FAN2).astype(BF16)
    out_ref[...] = (dot(hidden, w2_ref[0]) + dot(mean2, w2_ref[1])).astype(BF16)

    wait_in(10, gz_in.at[pl.ds(0, n_graph - 1)])
    gfin[sheet] = jnp.sum(gz_in[...], axis=0).astype(BF16)
    for _, graph, feat in sheet_peers:
        remote(11, gfin.at[sheet], gfin.at[sheet], graph, feat).start()

    wait_in(9, dw_in.at[pl.ds(0, n_row - 1)])
    dz[...] = jnp.sum(dw_in[...].astype(F32), axis=0)
    dz_in[g] = dz[...]
    for peer in graphs:
        remote(12, dz, dz_in.at[g], peer, f).start()
    wait_in(12, dz_in.at[pl.ds(0, n_graph - 1)])
    g1_ref[...] = jnp.sum(dz_in[...], axis=0).reshape(2, 8, HID)

    def unpack(ref, which):
        both = ref[...].astype(F32)
        g2_ref[which, :, 0:128] = both[:, :shard].reshape(HID, 128)
        g2_ref[which, :, 128:256] = both[:, shard:].reshape(HID, 128)

    wait_in(11, gfin.at[pl.ds(0, n_chip - 1)])
    remote(13, gfin, gsib, g, sibling).start()
    unpack(gfin, core)
    wait_in(13, gsib)
    unpack(gsib, 1 - core)

    wait_out(0, w_all.at[pl.ds(0, n_row - 1)])
    wait_out(1, x_all.at[pl.ds(0, n_row - 1)])
    wait_out(2, e_in.at[pl.ds(0, n_graph - 1)])
    wait_out(3, v_in)
    wait_out(4, pre_in.at[pl.ds(1, 3)])
    wait_out(5, hid_in)
    wait_out(6, d_all.at[pl.ds(0, 3)])
    wait_out(7, hh_in.at[pl.ds(0, n_graph - 1)])
    wait_out(8, gs_in.at[pl.ds(0, n_chip - 1)])
    wait_out(9, dw_in.at[pl.ds(0, n_row - 1)])
    wait_out(10, gz_in.at[pl.ds(0, n_graph - 1)])
    wait_out(11, gfin.at[pl.ds(0, n_chip - 1)])
    wait_out(12, dz_in.at[pl.ds(0, n_graph - 1)])
    wait_out(13, gsib)


def store_kernel(a_ref, b_ref, c_ref, a_out, b_out, c_out, sem):
    copies = [
        pltpu.make_async_copy(src, dst, sem.at[i])
        for i, (src, dst) in enumerate(((b_ref, b_out), (a_ref, a_out), (c_ref, c_out)))
    ]
    for copy in copies:
        copy.start()
    for copy in copies:
        copy.wait()


def solution(mesh):
    n_graph, n_feat = mesh.shape["graph"], mesh.shape["feat"]
    n_chip, n_row = n_feat // 2, n_feat // 4
    pack = 2 * HID // n_chip

    def body(features, w_first, w_second, cotangent, nbr_first, send_rows, nbr_second):
        vmem = pl.BlockSpec(memory_space=pltpu.VMEM)
        hbm = pl.BlockSpec(memory_space=pltpu.HBM)
        shapes = (
            jax.ShapeDtypeStruct((OWN, HID), BF16),
            jax.ShapeDtypeStruct((2, HID, HID), F32),
            jax.ShapeDtypeStruct((2, 8, HID), F32),
        )
        results = pl.pallas_call(
            functools.partial(kernel, n_graph, n_feat),
            out_shape=tuple(pltpu.VMEM(a.shape, a.dtype) for a in shapes),
            in_specs=[hbm] * 7,
            out_specs=(vmem,) * 3,
            scratch_shapes=[
                pltpu.VMEM((8, SRC), BF16),
                pltpu.VMEM((FAN1, n_feat * OWN), jnp.int32),
                pltpu.VMEM((2, HID, HID), BF16),
                pltpu.VMEM((OWN, HID), BF16),
                pltpu.VMEM((n_graph, HALO), jnp.int32),
                pltpu.VMEM((FAN2, OWN), jnp.int32),
                pltpu.VMEM((GROUPS * 8, LO), F32),
                pltpu.VMEM((n_row, 16, 128), BF16),
                pltpu.VMEM((n_row, 16, 128), BF16),
                pltpu.VMEM((n_row, 16, HID), BF16),
                pltpu.VMEM((4, OWN, HID), F32),
                pltpu.VMEM((4, OWN, HID), F32),
                pltpu.VMEM((4, OWN, HID), BF16),
                pltpu.VMEM((OWN, HID), BF16),
                pltpu.VMEM((OWN, HID), BF16),
                pltpu.VMEM((OWN, HID), BF16),
                pltpu.VMEM((OWN, HID), BF16),
                pltpu.VMEM((n_graph, HALO, HID), F32),
                pltpu.VMEM((n_graph, HALO, HID), F32),
                pltpu.VMEM((n_graph, HALO, HID), F32),
                pltpu.VMEM((n_graph, HALO, HID), F32),
                pltpu.VMEM((n_chip, pack, 128), BF16),
                pltpu.VMEM((n_chip, pack, 128), BF16),
                pltpu.VMEM((pack, 128), F32),
                pltpu.VMEM((n_graph, pack, 128), F32),
                pltpu.VMEM((n_chip, pack, 128), BF16),
                pltpu.VMEM((n_chip, pack, 128), BF16),
                pltpu.VMEM((n_row, 16, HID), BF16),
                pltpu.VMEM((n_row, 16, HID), BF16),
                pltpu.VMEM((16, HID), F32),
                pltpu.VMEM((n_graph, 16, HID), F32),
                pltpu.SemaphoreType.DMA((14,)),
                pltpu.SemaphoreType.DMA((14,)),
                pltpu.SemaphoreType.DMA((7,)),
            ],
            compiler_params=pltpu.CompilerParams(
                collective_id=0, has_side_effects=True, vmem_limit_bytes=40 * 1024 * 1024
            ),
        )(
            *(
                pltpu.with_memory_space_constraint(a, pltpu.HBM)
                for a in (
                    features.T,
                    w_first.reshape(16, HID),
                    w_second,
                    cotangent,
                    nbr_first.T,
                    send_rows.reshape(n_graph, HALO),
                    nbr_second.T,
                )
            )
        )
        return pl.pallas_call(
            store_kernel,
            out_shape=shapes,
            in_specs=[vmem] * 3,
            out_specs=(hbm,) * 3,
            scratch_shapes=[pltpu.SemaphoreType.DMA((3,))],
        )(*(pltpu.with_memory_space_constraint(a, pltpu.VMEM) for a in results))

    in_specs = (
        P("graph", "feat"),
        P(None, "feat", None),
        P(),
        P(("graph", "feat"), None),
        P("graph", None),
        P(("graph", "feat"), None, None),
        P(("graph", "feat"), None),
    )
    out_specs = (P(("graph", "feat"), None), P(), P(None, "feat", None))
    return jax.shard_map(body, mesh=mesh, in_specs=in_specs, out_specs=out_specs, check_vma=False)
```

```python
import functools

import jax
import jax.numpy as jnp
from jax import lax
from jax.experimental import pallas as pl
from jax.experimental.pallas import tpu as pltpu
from jax.sharding import PartitionSpec as P

HID = 256
FAN1 = 15
FAN2 = 10
OWN = 32
HALO = 8
SRC = 4096
N_X = 4
LO = 256
GROUPS = SRC // LO
BF16 = jnp.bfloat16
F32 = jnp.float32
MESH = pl.DeviceIdType.MESH


def select_tree(values, masks):
    for mask in masks:
        values = [
            jnp.where(mask, values[2 * i + 1], values[2 * i]) for i in range(len(values) // 2)
        ]
    return values[0]


def dot(a, b):
    return jnp.dot(a, b, preferred_element_type=F32)


def dot_lhs_t(a, b):
    return lax.dot_general(a, b, (((0,), (0,)), ((), ())), preferred_element_type=F32)


def dot_rhs_t(a, b):
    return lax.dot_general(a, b, (((1,), (1,)), ((), ())), preferred_element_type=F32)


def fold(a):
    return jnp.concatenate([a[:, :, :128], a[:, :, 128:]], axis=1)


def unfold(a):
    half = a.shape[1] // 2
    return jnp.concatenate([a[:, :half], a[:, half:]], axis=2)


def outward(n, i):
    return n // 2 + (1 - 2 * (i % 2)) * ((i + 1) // 2)


def split(a):
    high = a.astype(BF16)
    return high, (a - high.astype(F32)).astype(BF16)


def kernel(
    n_graph, n_feat,
    feat_hbm, w1_hbm, w2_hbm, cot_hbm, near1_hbm, send_hbm, near2_hbm,
    out_ref, g2_ref, g1_ref,
    feat_ref, near1_ref, w2_ref, cot_ref, send_ref, near2_ref,
    table, x_own, x_all, w_all, pre_own, pre_out, pre_in, d_all, hid_own, hid_in,
    v_out, v_in, e_out, e_in, hh_out, hh_in,
    gs_out, gs_in, gz, gz_in, gfin, gsib, dw_out, dw_in, dz, dz_in,
    send_sem, recv_sem, load_sem,
):
    n_chip = n_feat // 2
    n_y = n_chip // N_X
    n_block = 2 * N_X
    rows_x = 2 * n_y * OWN
    n_tiles = min(2, N_X)
    tile = N_X * rows_x // n_tiles
    shard = HID // n_chip
    g = lax.axis_index("graph")
    f = lax.axis_index("feat")
    chip, core = f // 2, f % 2
    x, y = chip // n_y, chip % n_y
    sibling = f + 1 - 2 * core
    block_own = 2 * x + core
    sheet = x * n_y + (1 - core) * y + core * g

    depth = (1 - core) * y + core * g
    around = (1 - core) * g + core * y
    turn_x = [(x + outward(N_X, i)) % N_X for i in range(N_X)]
    turn_d = [(depth + outward(n_y, i)) % n_y for i in range(n_y)]
    turn_a = [(around + outward(n_y, i)) % n_y for i in range(n_y)]
    graphs = [(g + outward(n_graph, i)) % n_graph for i in range(n_graph - 1)]
    sheet_x = [2 * n_y * to + core for to in turn_x]
    sheet_f = [2 * ((1 - core) * to + core * y) for to in turn_d]
    sheet_g = [(1 - core) * g + core * to for to in turn_d]
    sheet_peers = [
        (turn_x[i % N_X] * n_y + turn_d[i // N_X], sheet_g[i // N_X], sheet_x[i % N_X] + sheet_f[i // N_X])
        for i in range(n_chip - 1)
    ]
    ring_peers = [
        ((1 - core) * to + core * g, 2 * (x * n_y + (1 - core) * y + core * to) + core) for to in turn_a[:-1]
    ]
    block_peers = [
        (2 * to + other, 2 * (to * n_y + y) + other) for to in turn_x for other in (1 - core, core)
    ][:-1]
    column = [(y + outward(n_y, i)) % n_y for i in range(n_y - 1)]
    column_peers = [(to, 2 * (x * n_y + to) + core) for to in column]
    column_sources = [2 * (x * n_y + (y - outward(n_y, i) + n_y) % n_y) + core for i in range(n_y - 1)]

    def remote(index, src, dst, graph, feat):
        return pltpu.make_async_remote_copy(
            src_ref=src, dst_ref=dst, send_sem=send_sem.at[index], recv_sem=recv_sem.at[index],
            device_id=(graph, feat), device_id_type=MESH,
        )

    def wait_in(index, ref):
        remote(index, ref, ref, g, sibling).wait_recv()

    def wait_out(index, ref):
        remote(index, ref, ref, g, sibling).wait_send()

    loads = [
        pltpu.make_async_copy(src, dst, load_sem.at[i])
        for i, (src, dst) in enumerate((
            (feat_hbm, feat_ref), (near1_hbm, near1_ref), (w1_hbm, w_all.at[n_y - 1]), (cot_hbm, cot_ref),
            (near2_hbm, near2_ref), (send_hbm, send_ref), (w2_hbm, w2_ref),
        ))
    ]
    for load in loads:
        load.start()

    barrier = pltpu.get_barrier_semaphore()

    def greet(graph, feat):
        pl.semaphore_signal(barrier, inc=1, device_id=(graph, feat), device_id_type=MESH)

    for _, graph, feat in sheet_peers:
        greet(graph, feat)
    for graph, feat in ring_peers:
        greet(graph, feat)

    for i in range(0, n_block, 2):
        greet(g, block_peers[i][1])

    loads[0].wait()
    loads[1].wait()
    for s in range(GROUPS):
        table[s * 8 : (s + 1) * 8, :] = feat_ref[:, s * LO : (s + 1) * LO].astype(F32)
    lows = lax.broadcasted_iota(jnp.int32, (LO, tile), 0).astype(F32).astype(BF16)

    def gather(t):
        columns = pl.ds(pl.multiple_of(t * tile, tile), tile)
        near = near1_ref[:, columns]
        groups = table[...].astype(BF16)
        total = jnp.zeros((8, tile), F32)
        for k in range(FAN1):
            index = near[k : k + 1]
            low = jnp.broadcast_to((index % LO).astype(F32), (16, tile)).astype(BF16)
            low = jnp.concatenate([low] * (LO // 16), axis=0)
            picked = dot(groups, jnp.where(lows == low, jnp.ones((), BF16), jnp.zeros((), BF16)))
            high = jnp.broadcast_to(index // LO, (8, tile))
            masks = [(high // (1 << bit)) % 2 != 0 for bit in range(4)]
            total = total + select_tree([picked[s * 8 : (s + 1) * 8] for s in range(GROUPS)], masks)
        both = jnp.concatenate([feat_ref[:, columns].astype(F32), total / FAN1], axis=0).astype(BF16)
        for k in range(n_y):
            starts = [i * rows_x + 2 * k * OWN for i in range(tile // rows_x)]
            x_own[t, k] = jnp.concatenate([both[:, j : j + 2 * OWN] for j in starts], axis=1)

    def step(t, carry):
        gather(t)

        @pl.when(t == 0)
        def _():
            pl.semaphore_wait(barrier, n_chip - 1 + n_graph - 1 + N_X)
            loads[2].wait()
            own = w_all.at[n_y - 1]
            for i, (_, feat) in enumerate(column_peers):
                remote(0, own, w_all.at[i], g, feat).start()

        for i, (to, feat) in enumerate(column_peers):
            remote(14 + t, x_own.at[t, to], x_all.at[t, i], g, feat).start()
        x_all[t, n_y - 1] = x_own[t, y]
        return carry

    lax.fori_loop(0, n_tiles, step, 0)

    loads[3].wait()
    loads[4].wait()
    width = OWN + n_graph * HALO
    near2 = near2_ref[...]
    slots = lax.broadcasted_iota(jnp.int32, (width, OWN), 0)
    counts_t = jnp.zeros((width, OWN), F32)
    for k in range(FAN2):
        counts_t = counts_t + jnp.where(slots == near2[k : k + 1], 1.0, 0.0)
    counts_t = counts_t.astype(BF16)
    cot = cot_ref[...]
    e_all = dot(counts_t, cot)
    e_out[...] = fold(e_all[OWN:].reshape(n_graph, HALO, HID)).astype(BF16)
    for peer in graphs:
        remote(2, e_out.at[peer], e_in.at[g], peer, f).start()
    loads[5].wait()
    loads[6].wait()
    rows = lax.broadcasted_iota(jnp.int32, (OWN, n_graph * HALO), 0)
    sent = send_ref[...]
    sent = jnp.concatenate([sent[p : p + 1] for p in range(n_graph)], axis=1)
    pick_t = jnp.where(rows == sent, 1.0, 0.0).astype(BF16)

    wait_in(0, w_all.at[pl.ds(0, n_y - 1)])
    owners = n_block // n_tiles
    weights = w_all[...].reshape(n_y * 16, HID)
    inputs = []
    for t in range(n_tiles):
        wait_in(14 + t, x_all.at[t, pl.ds(0, n_y - 1)])
        inputs.append(x_all[t].reshape(n_y * 16, owners * OWN))
        sums = dot_lhs_t(inputs[t], weights).reshape(owners, OWN, HID)
        pre_own[t * owners : (t + 1) * owners] = sums
        pre_out[t * owners : (t + 1) * owners] = sums.astype(BF16)
        for i, (block, feat) in enumerate(block_peers):

            @pl.when(block // owners == t)
            def _(i=i, block=block, feat=feat):
                remote(4, pre_out.at[block], pre_in.at[i], g, feat).start()

    e_in[g] = jnp.zeros((2 * HALO, HID // 2), BF16)
    wait_in(2, e_in.at[pl.ds(0, n_graph - 1)])
    back = unfold(e_in[...].astype(F32)).reshape(n_graph * HALO, HID).astype(BF16)
    e_total = (e_all[:OWN] + dot(pick_t, back)) / FAN2
    e_high, e_low = split(e_total)
    first = jnp.broadcast_to(core, (OWN, HID)) == 0
    cot32, e32 = cot.astype(F32), e_high.astype(F32)
    v_own = jnp.where(first, cot32, e32).astype(BF16)
    v_out[...] = jnp.where(first, e32, cot32).astype(BF16)
    remote(3, v_out, v_in, g, sibling).start()
    d_hidden = dot_rhs_t(cot, w2_ref[0]) + (dot_rhs_t(e_high, w2_ref[1]) + dot_rhs_t(e_low, w2_ref[1]))

    wait_in(4, pre_in.at[pl.ds(0, n_block - 1)])
    pre = pre_own[block_own] + jnp.sum(pre_in[pl.ds(0, n_block - 1)].astype(F32), axis=0)
    sig = 1.0 / (1.0 + jnp.exp(-pre))
    hidden = (pre * sig).astype(BF16)
    hid_own[...] = hidden
    remote(5, hid_own, hid_in, g, sibling).start()
    d_all[block_own] = (d_hidden * (sig * (1.0 + pre * (1.0 - sig)))).astype(BF16)
    hh_out[...] = fold(dot_lhs_t(pick_t, hidden).reshape(n_graph, HALO, HID)).astype(BF16)

    wait_in(3, v_in)
    v_pair = jnp.concatenate([v_own, v_in[...]], axis=0)
    wait_in(5, hid_in)
    grad = dot_lhs_t(jnp.concatenate([hidden, hid_in[...]], axis=0), v_pair).reshape(n_chip, shard, HID)
    gs_out[...] = fold(grad).astype(BF16)

    for i, (peer, graph, feat) in enumerate(sheet_peers):
        remote(8, gs_out.at[peer], gs_in.at[i], graph, feat).start()
    gs_in[n_chip - 1] = gs_out[sheet]

    for _, feat in block_peers:
        remote(6, d_all.at[block_own], d_all.at[block_own], g, feat).start()
    for peer in graphs:
        remote(7, hh_out.at[peer], hh_in.at[g], peer, f).start()

    wait_in(8, gs_in.at[pl.ds(0, n_chip - 1)])
    gz[...] = jnp.sum(gs_in[...].astype(F32), axis=0)
    for graph, feat in ring_peers:
        remote(10, gz, gz_in.at[around], graph, feat).start()
    gz_in[around] = gz[...]

    wait_in(6, d_all.at[pl.ds(0, n_block - 1)])
    grad_rows = d_all[...].reshape(n_tiles, owners * OWN, HID)
    dw = sum(dot(inputs[t], grad_rows[t]) for t in range(n_tiles))
    dw_out[...] = dw.reshape(n_y, 16, HID).astype(BF16)
    for i, feat in enumerate(column_sources):
        remote(9, dw_out.at[i], dw_in.at[i], g, feat).start()
    dw_in[n_y - 1] = dw_out[n_y - 1]

    wait_in(10, gz_in.at[pl.ds(0, n_graph - 1)])
    gfin[sheet] = jnp.sum(gz_in[...], axis=0).astype(BF16)
    for _, graph, feat in sheet_peers:
        remote(11, gfin.at[sheet], gfin.at[sheet], graph, feat).start()

    wait_in(9, dw_in.at[pl.ds(0, n_y - 1)])
    dz[...] = jnp.sum(dw_in[...].astype(F32), axis=0).astype(BF16)
    for peer in graphs:
        remote(12, dz, dz_in.at[g], peer, f).start()
    dz_in[g] = dz[...]

    hh_in[g] = jnp.zeros((2 * HALO, HID // 2), BF16)
    wait_in(7, hh_in.at[pl.ds(0, n_graph - 1)])
    halo = unfold(hh_in[...].astype(F32)).reshape(n_graph * HALO, HID)
    ext = jnp.concatenate([hidden.astype(F32), halo], axis=0).astype(BF16)
    mean2 = (dot_lhs_t(counts_t, ext) / FAN2).astype(BF16)
    out_ref[...] = (dot(hidden, w2_ref[0]) + dot(mean2, w2_ref[1])).astype(BF16)

    def unpack(ref, which):
        both = ref[...].astype(F32)
        g2_ref[which, :, 0:128] = both[:, :shard].reshape(HID, 128)
        g2_ref[which, :, 128:256] = both[:, shard:].reshape(HID, 128)

    wait_in(11, gfin.at[pl.ds(0, n_chip - 1)])
    remote(13, gfin, gsib, g, sibling).start()
    unpack(gfin, core)
    wait_in(12, dz_in.at[pl.ds(0, n_graph - 1)])
    g1_ref[...] = jnp.sum(dz_in[...].astype(F32), axis=0).reshape(2, 8, HID)
    wait_in(13, gsib)
    unpack(gsib, 1 - core)

    wait_out(0, w_all.at[pl.ds(0, n_y - 1)])
    for t in range(n_tiles):
        wait_out(14 + t, x_all.at[t, pl.ds(0, n_y - 1)])
    wait_out(2, e_in.at[pl.ds(0, n_graph - 1)])
    wait_out(3, v_in)
    wait_out(4, pre_in.at[pl.ds(0, n_block - 1)])
    wait_out(5, hid_in)
    wait_out(6, d_all.at[pl.ds(0, n_block - 1)])
    wait_out(7, hh_in.at[pl.ds(0, n_graph - 1)])
    wait_out(8, gs_in.at[pl.ds(0, n_chip - 1)])
    wait_out(9, dw_in.at[pl.ds(0, n_y - 1)])
    wait_out(10, gz_in.at[pl.ds(0, n_graph - 1)])
    wait_out(11, gfin.at[pl.ds(0, n_chip - 1)])
    wait_out(12, dz_in.at[pl.ds(0, n_graph - 1)])
    wait_out(13, gsib)


def store_kernel(a_ref, b_ref, c_ref, a_out, b_out, c_out, sem):
    copies = [
        pltpu.make_async_copy(src, dst, sem.at[i])
        for i, (src, dst) in enumerate(((b_ref, b_out), (a_ref, a_out), (c_ref, c_out)))
    ]
    for copy in copies:
        copy.start()
    for copy in copies:
        copy.wait()


def solution(mesh):
    n_graph, n_feat = mesh.shape["graph"], mesh.shape["feat"]
    n_chip, n_block = n_feat // 2, 2 * N_X
    n_y, n_tiles = n_chip // N_X, min(2, N_X)
    pack = 2 * HID // n_chip

    def body(features, w_first, w_second, cotangent, nbr_first, send_rows, nbr_second):
        vmem = pl.BlockSpec(memory_space=pltpu.VMEM)
        hbm = pl.BlockSpec(memory_space=pltpu.HBM)
        shapes = (
            jax.ShapeDtypeStruct((OWN, HID), BF16),
            jax.ShapeDtypeStruct((2, HID, HID), F32),
            jax.ShapeDtypeStruct((2, 8, HID), F32),
        )
        results = pl.pallas_call(
            functools.partial(kernel, n_graph, n_feat),
            out_shape=tuple(pltpu.VMEM(a.shape, a.dtype) for a in shapes),
            in_specs=[hbm] * 7,
            out_specs=(vmem,) * 3,
            scratch_shapes=[
                pltpu.VMEM((8, SRC), BF16),
                pltpu.VMEM((FAN1, n_feat * OWN), jnp.int32),
                pltpu.VMEM((2, HID, HID), BF16),
                pltpu.VMEM((OWN, HID), BF16),
                pltpu.VMEM((n_graph, HALO), jnp.int32),
                pltpu.VMEM((FAN2, OWN), jnp.int32),
                pltpu.VMEM((GROUPS * 8, LO), F32),
                pltpu.VMEM((n_tiles, n_y, 16, n_block // n_tiles * OWN), BF16),
                pltpu.VMEM((n_tiles, n_y, 16, n_block // n_tiles * OWN), BF16),
                pltpu.VMEM((n_y, 16, HID), BF16),
                pltpu.VMEM((n_block, OWN, HID), F32),
                pltpu.VMEM((n_block, OWN, HID), BF16),
                pltpu.VMEM((n_block, OWN, HID), BF16),
                pltpu.VMEM((n_block, OWN, HID), BF16),
                pltpu.VMEM((OWN, HID), BF16),
                pltpu.VMEM((OWN, HID), BF16),
                pltpu.VMEM((OWN, HID), BF16),
                pltpu.VMEM((OWN, HID), BF16),
                pltpu.VMEM((n_graph, 2 * HALO, HID // 2), BF16),
                pltpu.VMEM((n_graph, 2 * HALO, HID // 2), BF16),
                pltpu.VMEM((n_graph, 2 * HALO, HID // 2), BF16),
                pltpu.VMEM((n_graph, 2 * HALO, HID // 2), BF16),
                pltpu.VMEM((n_chip, pack, 128), BF16),
                pltpu.VMEM((n_chip, pack, 128), BF16),
                pltpu.VMEM((pack, 128), F32),
                pltpu.VMEM((n_graph, pack, 128), F32),
                pltpu.VMEM((n_chip, pack, 128), BF16),
                pltpu.VMEM((n_chip, pack, 128), BF16),
                pltpu.VMEM((n_y, 16, HID), BF16),
                pltpu.VMEM((n_y, 16, HID), BF16),
                pltpu.VMEM((16, HID), BF16),
                pltpu.VMEM((n_graph, 16, HID), BF16),
                pltpu.SemaphoreType.DMA((16,)),
                pltpu.SemaphoreType.DMA((16,)),
                pltpu.SemaphoreType.DMA((7,)),
            ],
            compiler_params=pltpu.CompilerParams(
                collective_id=0, has_side_effects=True, vmem_limit_bytes=40 * 1024 * 1024
            ),
        )(
            *(
                pltpu.with_memory_space_constraint(a, pltpu.HBM)
                for a in (
                    features.T,
                    w_first.reshape(16, HID),
                    w_second,
                    cotangent,
                    nbr_first.T,
                    send_rows.reshape(n_graph, HALO),
                    nbr_second.T,
                )
            )
        )
        return pl.pallas_call(
            store_kernel,
            out_shape=shapes,
            in_specs=[vmem] * 3,
            out_specs=(hbm,) * 3,
            scratch_shapes=[pltpu.SemaphoreType.DMA((3,))],
        )(*(pltpu.with_memory_space_constraint(a, pltpu.VMEM) for a in results))

    in_specs = (
        P("graph", "feat"),
        P(None, "feat", None),
        P(),
        P(("graph", "feat"), None),
        P("graph", None),
        P(("graph", "feat"), None, None),
        P(("graph", "feat"), None),
    )
    out_specs = (P(("graph", "feat"), None), P(), P(None, "feat", None))
    return jax.shard_map(body, mesh=mesh, in_specs=in_specs, out_specs=out_specs, check_vma=False)
```

```python
import functools

import jax
import jax.numpy as jnp
from jax import lax
from jax.experimental import pallas as pl
from jax.experimental.pallas import tpu as pltpu
from jax.sharding import PartitionSpec as P

HID = 256
FAN1 = 15
FAN2 = 10
OWN = 32
HALO = 8
SRC = 4096
N_X = 4
LO = 256
GROUPS = SRC // LO
BF16 = jnp.bfloat16
F32 = jnp.float32
MESH = pl.DeviceIdType.MESH


def select_tree(values, masks):
    for mask in masks:
        values = [
            jnp.where(mask, values[2 * i + 1], values[2 * i]) for i in range(len(values) // 2)
        ]
    return values[0]


def dot(a, b):
    return jnp.dot(a, b, preferred_element_type=F32)


def dot_lhs_t(a, b):
    return lax.dot_general(a, b, (((0,), (0,)), ((), ())), preferred_element_type=F32)


def dot_rhs_t(a, b):
    return lax.dot_general(a, b, (((1,), (1,)), ((), ())), preferred_element_type=F32)


def fold(a):
    return jnp.concatenate([a[:, :, :128], a[:, :, 128:]], axis=1)


def unfold(a):
    half = a.shape[1] // 2
    return jnp.concatenate([a[:, :half], a[:, half:]], axis=2)


def outward(n, i):
    return n // 2 + (1 - 2 * (i % 2)) * ((i + 1) // 2)


def split(a):
    high = a.astype(BF16)
    return high, (a - high.astype(F32)).astype(BF16)


def kernel(
    n_graph, n_feat,
    feat_hbm, w1_hbm, w2_hbm, cot_hbm, near1_hbm, send_hbm, near2_hbm,
    out_ref, g2_ref, g1_ref,
    feat_ref, near1_ref, w2_ref, cot_ref, send_ref, near2_ref,
    table, x_own, x_all, w_all, pre_own, pre_out, pre_in, d_all,
    v_out, v_in, e_out, e_in, hh_out, hh_in,
    gs_out, gs_in, gz, gz_in, gfin, gsib, dw_out, dw_in, dz, dz_in,
    send_sem, recv_sem, load_sem,
):
    n_chip = n_feat // 2
    n_y = n_chip // N_X
    n_block = 2 * N_X
    rows_x = 2 * n_y * OWN
    n_tiles = min(2, N_X)
    tile = N_X * rows_x // n_tiles
    shard = HID // n_chip
    g = lax.axis_index("graph")
    f = lax.axis_index("feat")
    chip, core = f // 2, f % 2
    x, y = chip // n_y, chip % n_y
    sibling = f + 1 - 2 * core
    block_own = 2 * x + core
    sheet = x * n_y + (1 - core) * y + core * g

    depth = (1 - core) * y + core * g
    around = (1 - core) * g + core * y
    turn_x = [(x + outward(N_X, i)) % N_X for i in range(N_X)]
    turn_d = [(depth + outward(n_y, i)) % n_y for i in range(n_y)]
    turn_a = [(around + outward(n_y, i)) % n_y for i in range(n_y)]
    graphs = [(g + outward(n_graph, i)) % n_graph for i in range(n_graph - 1)]
    sheet_x = [2 * n_y * to + core for to in turn_x]
    sheet_f = [2 * ((1 - core) * to + core * y) for to in turn_d]
    sheet_g = [(1 - core) * g + core * to for to in turn_d]
    sheet_peers = [
        (turn_x[i % N_X] * n_y + turn_d[i // N_X], sheet_g[i // N_X], sheet_x[i % N_X] + sheet_f[i // N_X])
        for i in range(n_chip - 1)
    ]
    ring_peers = [
        ((1 - core) * to + core * g, 2 * (x * n_y + (1 - core) * y + core * to) + core) for to in turn_a[:-1]
    ]
    block_peers = [
        (2 * to + other, 2 * (to * n_y + y) + other) for to in turn_x for other in (1 - core, core)
    ][:-1]
    column = [(y + outward(n_y, i)) % n_y for i in range(n_y - 1)]
    column_peers = [(to, 2 * (x * n_y + to) + core) for to in column]
    column_sources = [2 * (x * n_y + (y - outward(n_y, i) + n_y) % n_y) + core for i in range(n_y - 1)]

    def remote(index, src, dst, graph, feat):
        return pltpu.make_async_remote_copy(
            src_ref=src, dst_ref=dst, send_sem=send_sem.at[index], recv_sem=recv_sem.at[index],
            device_id=(graph, feat), device_id_type=MESH,
        )

    def wait_in(index, ref):
        remote(index, ref, ref, g, sibling).wait_recv()

    def wait_out(index, ref):
        remote(index, ref, ref, g, sibling).wait_send()

    loads = [
        pltpu.make_async_copy(src, dst, load_sem.at[i])
        for i, (src, dst) in enumerate((
            (feat_hbm, feat_ref), (near1_hbm, near1_ref), (w1_hbm, w_all.at[n_y - 1]), (cot_hbm, cot_ref),
            (near2_hbm, near2_ref), (send_hbm, send_ref), (w2_hbm, w2_ref),
        ))
    ]
    for load in loads:
        load.start()

    barrier = pltpu.get_barrier_semaphore()

    def greet(graph, feat):
        pl.semaphore_signal(barrier, inc=1, device_id=(graph, feat), device_id_type=MESH)

    for _, graph, feat in sheet_peers:
        greet(graph, feat)
    for graph, feat in ring_peers:
        greet(graph, feat)

    for i in range(0, n_block, 2):
        greet(g, block_peers[i][1])

    loads[0].wait()
    loads[1].wait()
    for s in range(GROUPS):
        table[s * 8 : (s + 1) * 8, :] = feat_ref[:, s * LO : (s + 1) * LO].astype(F32)
    lows = lax.broadcasted_iota(jnp.int32, (LO, tile), 0).astype(F32).astype(BF16)

    def gather(t):
        columns = pl.ds(pl.multiple_of(t * tile, tile), tile)
        near = near1_ref[:, columns]
        groups = table[...].astype(BF16)
        total = jnp.zeros((8, tile), F32)
        for k in range(FAN1):
            index = near[k : k + 1]
            low = jnp.broadcast_to((index % LO).astype(F32), (16, tile)).astype(BF16)
            low = jnp.concatenate([low] * (LO // 16), axis=0)
            picked = dot(groups, jnp.where(lows == low, jnp.ones((), BF16), jnp.zeros((), BF16)))
            high = jnp.broadcast_to(index // LO, (8, tile))
            masks = [(high // (1 << bit)) % 2 != 0 for bit in range(4)]
            total = total + select_tree([picked[s * 8 : (s + 1) * 8] for s in range(GROUPS)], masks)
        both = jnp.concatenate([feat_ref[:, columns].astype(F32), total / FAN1], axis=0).astype(BF16)
        for k in range(n_y):
            starts = [i * rows_x + 2 * k * OWN for i in range(tile // rows_x)]
            x_own[t, k] = jnp.concatenate([both[:, j : j + 2 * OWN] for j in starts], axis=1)

    def step(t, carry):
        gather(t)

        @pl.when(t == 0)
        def _():
            pl.semaphore_wait(barrier, n_chip - 1 + n_graph - 1 + N_X)
            loads[2].wait()
            own = w_all.at[n_y - 1]
            for i, (_, feat) in enumerate(column_peers):
                remote(0, own, w_all.at[i], g, feat).start()

        for i, (to, feat) in enumerate(column_peers):
            remote(14 + t, x_own.at[t, to], x_all.at[t, i], g, feat).start()
        x_all[t, n_y - 1] = x_own[t, y]
        return carry

    lax.fori_loop(0, n_tiles, step, 0)

    loads[3].wait()
    loads[4].wait()
    width = OWN + n_graph * HALO
    near2 = near2_ref[...]
    slots = lax.broadcasted_iota(jnp.int32, (width, OWN), 0)
    counts_t = jnp.zeros((width, OWN), F32)
    for k in range(FAN2):
        counts_t = counts_t + jnp.where(slots == near2[k : k + 1], 1.0, 0.0)
    counts_t = counts_t.astype(BF16)
    cot = cot_ref[...]
    e_all = dot(counts_t, cot)
    e_out[...] = fold(e_all[OWN:].reshape(n_graph, HALO, HID)).astype(BF16)
    for peer in graphs:
        remote(2, e_out.at[peer], e_in.at[g], peer, f).start()
    loads[5].wait()
    loads[6].wait()
    rows = lax.broadcasted_iota(jnp.int32, (OWN, n_graph * HALO), 0)
    sent = send_ref[...]
    sent = jnp.concatenate([sent[p : p + 1] for p in range(n_graph)], axis=1)
    pick_t = jnp.where(rows == sent, 1.0, 0.0).astype(BF16)

    wait_in(0, w_all.at[pl.ds(0, n_y - 1)])
    owners = n_block // n_tiles
    weights = w_all[...].reshape(n_y * 16, HID)
    inputs = []
    for t in range(n_tiles):
        wait_in(14 + t, x_all.at[t, pl.ds(0, n_y - 1)])
        inputs.append(x_all[t].reshape(n_y * 16, owners * OWN))
        sums = dot_lhs_t(inputs[t], weights).reshape(owners, OWN, HID)
        pre_own[t * owners : (t + 1) * owners] = sums
        pre_out[t * owners : (t + 1) * owners] = sums.astype(BF16)
        for i, (block, feat) in enumerate(block_peers):

            @pl.when(block // owners == t)
            def _(i=i, block=block, feat=feat):
                remote(4, pre_out.at[pl.ds(block // 2 * 2, 2)], pre_in.at[pl.ds(2 * i, 2)], g, feat).start()

    e_in[g] = jnp.zeros((2 * HALO, HID // 2), BF16)
    wait_in(2, e_in.at[pl.ds(0, n_graph - 1)])
    back = unfold(e_in[...].astype(F32)).reshape(n_graph * HALO, HID).astype(BF16)
    e_total = (e_all[:OWN] + dot(pick_t, back)) / FAN2
    e_high, e_low = split(e_total)
    first = jnp.broadcast_to(core, (OWN, HID)) == 0
    cot32, e32 = cot.astype(F32), e_high.astype(F32)
    v_own = jnp.where(first, cot32, e32).astype(BF16)
    v_out[...] = jnp.where(first, e32, cot32).astype(BF16)
    remote(3, v_out, v_in, g, sibling).start()
    d_hidden = dot_rhs_t(cot, w2_ref[0]) + (dot_rhs_t(e_high, w2_ref[1]) + dot_rhs_t(e_low, w2_ref[1]))

    wait_in(4, pre_in.at[pl.ds(0, 2 * n_block - 2)])
    pair = (n_block - 1, 2, OWN, HID)
    pre_both = pre_own[pl.ds(2 * x, 2)] + jnp.sum(pre_in[pl.ds(0, 2 * n_block - 2)].astype(F32).reshape(pair), axis=0)
    hid_both = (pre_both * (1.0 / (1.0 + jnp.exp(-pre_both)))).astype(BF16)
    pre = jnp.where(first, pre_both[0], pre_both[1])
    sig = 1.0 / (1.0 + jnp.exp(-pre))
    hidden = (pre * sig).astype(BF16)
    d_all[block_own] = (d_hidden * (sig * (1.0 + pre * (1.0 - sig)))).astype(BF16)
    hh_out[...] = fold(dot_lhs_t(pick_t, hidden).reshape(n_graph, HALO, HID)).astype(BF16)

    wait_in(3, v_in)
    v_own32, v_in32 = v_own.astype(F32), v_in[...].astype(F32)
    v_pair = jnp.concatenate([jnp.where(first, v_own32, v_in32), jnp.where(first, v_in32, v_own32)], axis=0).astype(BF16)
    grad = dot_lhs_t(hid_both.reshape(2 * OWN, HID), v_pair).reshape(n_chip, shard, HID)
    gs_out[...] = fold(grad).astype(BF16)

    for i, (peer, graph, feat) in enumerate(sheet_peers):
        remote(8, gs_out.at[peer], gs_in.at[i], graph, feat).start()
    gs_in[n_chip - 1] = gs_out[sheet]

    for _, feat in block_peers:
        remote(6, d_all.at[block_own], d_all.at[block_own], g, feat).start()
    for peer in graphs:
        remote(7, hh_out.at[peer], hh_in.at[g], peer, f).start()

    wait_in(8, gs_in.at[pl.ds(0, n_chip - 1)])
    gz[...] = jnp.sum(gs_in[...].astype(F32), axis=0)
    for graph, feat in ring_peers:
        remote(10, gz, gz_in.at[around], graph, feat).start()
    gz_in[around] = gz[...]

    wait_in(6, d_all.at[pl.ds(0, n_block - 1)])
    grad_rows = d_all[...].reshape(n_tiles, owners * OWN, HID)
    dw = sum(dot(inputs[t], grad_rows[t]) for t in range(n_tiles))
    dw_out[...] = dw.reshape(n_y, 16, HID).astype(BF16)
    for i, feat in enumerate(column_sources):
        remote(9, dw_out.at[i], dw_in.at[i], g, feat).start()
    dw_in[n_y - 1] = dw_out[n_y - 1]

    wait_in(10, gz_in.at[pl.ds(0, n_graph - 1)])
    gfin[sheet] = jnp.sum(gz_in[...], axis=0).astype(BF16)
    for _, graph, feat in sheet_peers:
        remote(11, gfin.at[sheet], gfin.at[sheet], graph, feat).start()

    wait_in(9, dw_in.at[pl.ds(0, n_y - 1)])
    dz[...] = jnp.sum(dw_in[...].astype(F32), axis=0).astype(BF16)
    for peer in graphs:
        remote(12, dz, dz_in.at[g], peer, f).start()
    dz_in[g] = dz[...]

    hh_in[g] = jnp.zeros((2 * HALO, HID // 2), BF16)
    wait_in(7, hh_in.at[pl.ds(0, n_graph - 1)])
    halo = unfold(hh_in[...].astype(F32)).reshape(n_graph * HALO, HID)
    ext = jnp.concatenate([hidden.astype(F32), halo], axis=0).astype(BF16)
    mean2 = (dot_lhs_t(counts_t, ext) / FAN2).astype(BF16)
    out_ref[...] = (dot(hidden, w2_ref[0]) + dot(mean2, w2_ref[1])).astype(BF16)

    def unpack(ref, which):
        both = ref[...].astype(F32)
        g2_ref[which, :, 0:128] = both[:, :shard].reshape(HID, 128)
        g2_ref[which, :, 128:256] = both[:, shard:].reshape(HID, 128)

    wait_in(11, gfin.at[pl.ds(0, n_chip - 1)])
    remote(13, gfin, gsib, g, sibling).start()
    unpack(gfin, core)
    wait_in(12, dz_in.at[pl.ds(0, n_graph - 1)])
    g1_ref[...] = jnp.sum(dz_in[...].astype(F32), axis=0).reshape(2, 8, HID)
    wait_in(13, gsib)
    unpack(gsib, 1 - core)

    wait_out(0, w_all.at[pl.ds(0, n_y - 1)])
    for t in range(n_tiles):
        wait_out(14 + t, x_all.at[t, pl.ds(0, n_y - 1)])
    wait_out(2, e_in.at[pl.ds(0, n_graph - 1)])
    wait_out(3, v_in)
    wait_out(4, pre_in.at[pl.ds(0, 2 * n_block - 2)])
    wait_out(6, d_all.at[pl.ds(0, n_block - 1)])
    wait_out(7, hh_in.at[pl.ds(0, n_graph - 1)])
    wait_out(8, gs_in.at[pl.ds(0, n_chip - 1)])
    wait_out(9, dw_in.at[pl.ds(0, n_y - 1)])
    wait_out(10, gz_in.at[pl.ds(0, n_graph - 1)])
    wait_out(11, gfin.at[pl.ds(0, n_chip - 1)])
    wait_out(12, dz_in.at[pl.ds(0, n_graph - 1)])
    wait_out(13, gsib)


def store_kernel(a_ref, b_ref, c_ref, a_out, b_out, c_out, sem):
    copies = [
        pltpu.make_async_copy(src, dst, sem.at[i])
        for i, (src, dst) in enumerate(((b_ref, b_out), (a_ref, a_out), (c_ref, c_out)))
    ]
    for copy in copies:
        copy.start()
    for copy in copies:
        copy.wait()


def solution(mesh):
    n_graph, n_feat = mesh.shape["graph"], mesh.shape["feat"]
    n_chip, n_block = n_feat // 2, 2 * N_X
    n_y, n_tiles = n_chip // N_X, min(2, N_X)
    pack = 2 * HID // n_chip

    def body(features, w_first, w_second, cotangent, nbr_first, send_rows, nbr_second):
        vmem = pl.BlockSpec(memory_space=pltpu.VMEM)
        hbm = pl.BlockSpec(memory_space=pltpu.HBM)
        shapes = (
            jax.ShapeDtypeStruct((OWN, HID), BF16),
            jax.ShapeDtypeStruct((2, HID, HID), F32),
            jax.ShapeDtypeStruct((2, 8, HID), F32),
        )
        results = pl.pallas_call(
            functools.partial(kernel, n_graph, n_feat),
            out_shape=tuple(pltpu.VMEM(a.shape, a.dtype) for a in shapes),
            in_specs=[hbm] * 7,
            out_specs=(vmem,) * 3,
            scratch_shapes=[
                pltpu.VMEM((8, SRC), BF16),
                pltpu.VMEM((FAN1, n_feat * OWN), jnp.int32),
                pltpu.VMEM((2, HID, HID), BF16),
                pltpu.VMEM((OWN, HID), BF16),
                pltpu.VMEM((n_graph, HALO), jnp.int32),
                pltpu.VMEM((FAN2, OWN), jnp.int32),
                pltpu.VMEM((GROUPS * 8, LO), F32),
                pltpu.VMEM((n_tiles, n_y, 16, n_block // n_tiles * OWN), BF16),
                pltpu.VMEM((n_tiles, n_y, 16, n_block // n_tiles * OWN), BF16),
                pltpu.VMEM((n_y, 16, HID), BF16),
                pltpu.VMEM((n_block, OWN, HID), F32),
                pltpu.VMEM((n_block, OWN, HID), BF16),
                pltpu.VMEM((2 * n_block, OWN, HID), BF16),
                pltpu.VMEM((n_block, OWN, HID), BF16),
                pltpu.VMEM((OWN, HID), BF16),
                pltpu.VMEM((OWN, HID), BF16),
                pltpu.VMEM((n_graph, 2 * HALO, HID // 2), BF16),
                pltpu.VMEM((n_graph, 2 * HALO, HID // 2), BF16),
                pltpu.VMEM((n_graph, 2 * HALO, HID // 2), BF16),
                pltpu.VMEM((n_graph, 2 * HALO, HID // 2), BF16),
                pltpu.VMEM((n_chip, pack, 128), BF16),
                pltpu.VMEM((n_chip, pack, 128), BF16),
                pltpu.VMEM((pack, 128), F32),
                pltpu.VMEM((n_graph, pack, 128), F32),
                pltpu.VMEM((n_chip, pack, 128), BF16),
                pltpu.VMEM((n_chip, pack, 128), BF16),
                pltpu.VMEM((n_y, 16, HID), BF16),
                pltpu.VMEM((n_y, 16, HID), BF16),
                pltpu.VMEM((16, HID), BF16),
                pltpu.VMEM((n_graph, 16, HID), BF16),
                pltpu.SemaphoreType.DMA((16,)),
                pltpu.SemaphoreType.DMA((16,)),
                pltpu.SemaphoreType.DMA((7,)),
            ],
            compiler_params=pltpu.CompilerParams(
                collective_id=0, has_side_effects=True, vmem_limit_bytes=40 * 1024 * 1024
            ),
        )(
            *(
                pltpu.with_memory_space_constraint(a, pltpu.HBM)
                for a in (
                    features.T,
                    w_first.reshape(16, HID),
                    w_second,
                    cotangent,
                    nbr_first.T,
                    send_rows.reshape(n_graph, HALO),
                    nbr_second.T,
                )
            )
        )
        return pl.pallas_call(
            store_kernel,
            out_shape=shapes,
            in_specs=[vmem] * 3,
            out_specs=(hbm,) * 3,
            scratch_shapes=[pltpu.SemaphoreType.DMA((3,))],
        )(*(pltpu.with_memory_space_constraint(a, pltpu.VMEM) for a in results))

    in_specs = (
        P("graph", "feat"),
        P(None, "feat", None),
        P(),
        P(("graph", "feat"), None),
        P("graph", None),
        P(("graph", "feat"), None, None),
        P(("graph", "feat"), None),
    )
    out_specs = (P(("graph", "feat"), None), P(), P(None, "feat", None))
    return jax.shard_map(body, mesh=mesh, in_specs=in_specs, out_specs=out_specs, check_vma=False)
```

```python
import functools

import jax
import jax.numpy as jnp
from jax import lax
from jax.experimental import pallas as pl
from jax.experimental.pallas import tpu as pltpu
from jax.sharding import PartitionSpec as P

HID = 256
FAN1 = 15
FAN2 = 10
OWN = 32
HALO = 8
SRC = 4096
N_X = 4
LO = 256
GROUPS = SRC // LO
BF16 = jnp.bfloat16
F32 = jnp.float32
MESH = pl.DeviceIdType.MESH


def select_tree(values, masks):
    for mask in masks:
        values = [
            jnp.where(mask, values[2 * i + 1], values[2 * i]) for i in range(len(values) // 2)
        ]
    return values[0]


def dot(a, b):
    return jnp.dot(a, b, preferred_element_type=F32)


def dot_lhs_t(a, b):
    return lax.dot_general(a, b, (((0,), (0,)), ((), ())), preferred_element_type=F32)


def dot_rhs_t(a, b):
    return lax.dot_general(a, b, (((1,), (1,)), ((), ())), preferred_element_type=F32)


def fold(a):
    return jnp.concatenate([a[:, :, :128], a[:, :, 128:]], axis=1)


def unfold(a):
    half = a.shape[1] // 2
    return jnp.concatenate([a[:, :half], a[:, half:]], axis=2)


def outward(n, i):
    return n // 2 + (1 - 2 * (i % 2)) * ((i + 1) // 2)


def split(a):
    high = a.astype(BF16)
    return high, (a - high.astype(F32)).astype(BF16)


def kernel(
    n_graph, n_feat,
    feat_hbm, w1_hbm, w2_hbm, cot_hbm, near1_hbm, send_hbm, near2_hbm,
    out_ref, g2_ref, g1_ref,
    feat_ref, near1_ref, w2_ref, cot_ref, send_ref, near2_ref,
    table, x_own, x_all, w_all, pre_own, pre_out, pre_in, d_all, hid_own, hid_in,
    v_out, v_in, e_out, e_in, hh_out, hh_in,
    gs_out, gs_in, gz, gz_in, gfin, gsib, dw_out, dw_in, dz, dz_in,
    send_sem, recv_sem, load_sem,
):
    n_chip = n_feat // 2
    n_y = n_chip // N_X
    n_block = 2 * N_X
    rows_x = 2 * n_y * OWN
    n_tiles = min(2, N_X)
    tile = N_X * rows_x // n_tiles
    shard = HID // n_chip
    g = lax.axis_index("graph")
    f = lax.axis_index("feat")
    chip, core = f // 2, f % 2
    x, y = chip // n_y, chip % n_y
    sibling = f + 1 - 2 * core
    block_own = 2 * x + core
    sheet = x * n_y + (1 - core) * y + core * g

    depth = (1 - core) * y + core * g
    around = (1 - core) * g + core * y
    turn_x = [(x + outward(N_X, i)) % N_X for i in range(N_X)]
    turn_d = [(depth + outward(n_y, i)) % n_y for i in range(n_y)]
    turn_a = [(around + outward(n_y, i)) % n_y for i in range(n_y)]
    graphs = [(g + outward(n_graph, i)) % n_graph for i in range(n_graph - 1)]
    sheet_x = [2 * n_y * to + core for to in turn_x]
    sheet_f = [2 * ((1 - core) * to + core * y) for to in turn_d]
    sheet_g = [(1 - core) * g + core * to for to in turn_d]
    sheet_peers = [
        (turn_x[i % N_X] * n_y + turn_d[i // N_X], sheet_g[i // N_X], sheet_x[i % N_X] + sheet_f[i // N_X])
        for i in range(n_chip - 1)
    ]
    ring_peers = [
        ((1 - core) * to + core * g, 2 * (x * n_y + (1 - core) * y + core * to) + core) for to in turn_a[:-1]
    ]
    block_peers = [
        (2 * to + other, 2 * (to * n_y + y) + other) for to in turn_x for other in (1 - core, core)
    ][:-1]
    column = [(y + outward(n_y, i)) % n_y for i in range(n_y - 1)]
    column_peers = [(to, 2 * (x * n_y + to) + core) for to in column]
    column_sources = [2 * (x * n_y + (y - outward(n_y, i) + n_y) % n_y) + core for i in range(n_y - 1)]

    def remote(index, src, dst, graph, feat):
        return pltpu.make_async_remote_copy(
            src_ref=src, dst_ref=dst, send_sem=send_sem.at[index], recv_sem=recv_sem.at[index],
            device_id=(graph, feat), device_id_type=MESH,
        )

    def wait_in(index, ref):
        remote(index, ref, ref, g, sibling).wait_recv()

    def wait_out(index, ref):
        remote(index, ref, ref, g, sibling).wait_send()

    loads = [
        pltpu.make_async_copy(src, dst, load_sem.at[i])
        for i, (src, dst) in enumerate((
            (feat_hbm, feat_ref), (near1_hbm, near1_ref), (w1_hbm, w_all.at[n_y - 1]), (cot_hbm, cot_ref),
            (near2_hbm, near2_ref), (send_hbm, send_ref), (w2_hbm, w2_ref),
        ))
    ]
    for load in loads:
        load.start()

    barrier = pltpu.get_barrier_semaphore()

    def greet(graph, feat):
        pl.semaphore_signal(barrier, inc=1, device_id=(graph, feat), device_id_type=MESH)

    for _, graph, feat in sheet_peers:
        greet(graph, feat)
    for graph, feat in ring_peers:
        greet(graph, feat)

    for i in range(0, n_block, 2):
        greet(g, block_peers[i][1])

    loads[0].wait()
    loads[1].wait()
    for s in range(GROUPS):
        table[s * 8 : (s + 1) * 8, :] = feat_ref[:, s * LO : (s + 1) * LO].astype(F32)
    lows = lax.broadcasted_iota(jnp.int32, (LO, tile), 0).astype(F32).astype(BF16)

    def gather(t):
        columns = pl.ds(pl.multiple_of(t * tile, tile), tile)
        near = near1_ref[:, columns]
        groups = table[...].astype(BF16)
        total = jnp.zeros((8, tile), F32)
        for k in range(FAN1):
            index = near[k : k + 1]
            low = jnp.broadcast_to((index % LO).astype(F32), (16, tile)).astype(BF16)
            low = jnp.concatenate([low] * (LO // 16), axis=0)
            picked = dot(groups, jnp.where(lows == low, jnp.ones((), BF16), jnp.zeros((), BF16)))
            high = jnp.broadcast_to(index // LO, (8, tile))
            masks = [(high // (1 << bit)) % 2 != 0 for bit in range(4)]
            total = total + select_tree([picked[s * 8 : (s + 1) * 8] for s in range(GROUPS)], masks)
        both = jnp.concatenate([feat_ref[:, columns].astype(F32), total / FAN1], axis=0).astype(BF16)
        for k in range(n_y):
            starts = [i * rows_x + 2 * k * OWN for i in range(tile // rows_x)]
            x_own[t, k] = jnp.concatenate([both[:, j : j + 2 * OWN] for j in starts], axis=1)

    def step(t, carry):
        gather(t)

        @pl.when(t == 0)
        def _():
            pl.semaphore_wait(barrier, n_chip - 1 + n_graph - 1 + N_X)
            loads[2].wait()
            own = w_all.at[n_y - 1]
            for i, (_, feat) in enumerate(column_peers):
                remote(0, own, w_all.at[i], g, feat).start()

        for i, (to, feat) in enumerate(column_peers):
            remote(14 + t, x_own.at[t, to], x_all.at[t, i], g, feat).start()
        x_all[t, n_y - 1] = x_own[t, y]
        return carry

    lax.fori_loop(0, n_tiles, step, 0)

    loads[3].wait()
    loads[4].wait()
    width = OWN + n_graph * HALO
    near2 = near2_ref[...]
    slots = lax.broadcasted_iota(jnp.int32, (width, OWN), 0)
    counts_t = jnp.zeros((width, OWN), F32)
    for k in range(FAN2):
        counts_t = counts_t + jnp.where(slots == near2[k : k + 1], 1.0, 0.0)
    counts_t = counts_t.astype(BF16)
    cot = cot_ref[...]
    e_all = dot(counts_t, cot)
    e_out[...] = fold(e_all[OWN:].reshape(n_graph, HALO, HID)).astype(BF16)
    for peer in graphs:
        remote(2, e_out.at[peer], e_in.at[g], peer, f).start()
    loads[5].wait()
    loads[6].wait()
    rows = lax.broadcasted_iota(jnp.int32, (OWN, n_graph * HALO), 0)
    sent = send_ref[...]
    sent = jnp.concatenate([sent[p : p + 1] for p in range(n_graph)], axis=1)
    pick_t = jnp.where(rows == sent, 1.0, 0.0).astype(BF16)

    wait_in(0, w_all.at[pl.ds(0, n_y - 1)])
    owners = n_block // n_tiles
    weights = w_all[...].reshape(n_y * 16, HID)
    inputs = []
    for t in range(n_tiles):
        wait_in(14 + t, x_all.at[t, pl.ds(0, n_y - 1)])
        inputs.append(x_all[t].reshape(n_y * 16, owners * OWN))
        sums = dot_lhs_t(inputs[t], weights).reshape(owners, OWN, HID)
        pre_own[t * owners : (t + 1) * owners] = sums
        pre_out[t * owners : (t + 1) * owners] = sums.astype(BF16)
        for i, (block, feat) in enumerate(block_peers):

            @pl.when(block // owners == t)
            def _(i=i, block=block, feat=feat):
                remote(4, pre_out.at[block], pre_in.at[i], g, feat).start()

    e_in[g] = jnp.zeros((2 * HALO, HID // 2), BF16)
    wait_in(2, e_in.at[pl.ds(0, n_graph - 1)])
    back = unfold(e_in[...].astype(F32)).reshape(n_graph * HALO, HID).astype(BF16)
    e_total = (e_all[:OWN] + dot(pick_t, back)) / FAN2
    e_high, e_low = split(e_total)
    first = jnp.broadcast_to(core, (OWN, HID)) == 0
    cot32, e32 = cot.astype(F32), e_high.astype(F32)
    v_own = jnp.where(first, cot32, e32).astype(BF16)
    v_out[...] = jnp.where(first, e32, cot32).astype(BF16)
    remote(3, v_out, v_in, g, sibling).start()
    d_hidden = dot_rhs_t(cot, w2_ref[0]) + (dot_rhs_t(e_high, w2_ref[1]) + dot_rhs_t(e_low, w2_ref[1]))

    wait_in(4, pre_in.at[pl.ds(0, n_block - 1)])
    pre = pre_own[block_own] + jnp.sum(pre_in[pl.ds(0, n_block - 1)].astype(F32), axis=0)
    sig = 1.0 / (1.0 + jnp.exp(-pre))
    hidden = (pre * sig).astype(BF16)
    hid_own[...] = hidden
    remote(5, hid_own, hid_in, g, sibling).start()
    d_all[block_own] = (d_hidden * (sig * (1.0 + pre * (1.0 - sig)))).astype(BF16)
    hh_out[...] = fold(dot_lhs_t(pick_t, hidden).reshape(n_graph, HALO, HID)).astype(BF16)

    wait_in(3, v_in)
    v_pair = jnp.concatenate([v_own, v_in[...]], axis=0)
    wait_in(5, hid_in)
    grad = dot_lhs_t(jnp.concatenate([hidden, hid_in[...]], axis=0), v_pair).reshape(n_chip, shard, HID)
    gs_out[...] = fold(grad).astype(BF16)

    for i, (peer, graph, feat) in enumerate(sheet_peers):
        remote(8, gs_out.at[peer], gs_in.at[i], graph, feat).start()
    gs_in[n_chip - 1] = gs_out[sheet]

    for _, feat in block_peers:
        remote(6, d_all.at[block_own], d_all.at[block_own], g, feat).start()
    for peer in graphs:
        remote(7, hh_out.at[peer], hh_in.at[g], peer, f).start()

    wait_in(8, gs_in.at[pl.ds(0, n_chip - 1)])
    gz[...] = jnp.sum(gs_in[...].astype(F32), axis=0)
    for graph, feat in ring_peers:
        remote(10, gz, gz_in.at[around], graph, feat).start()
    gz_in[around] = gz[...]

    wait_in(6, d_all.at[pl.ds(0, n_block - 1)])
    grad_rows = d_all[...].reshape(n_tiles, owners * OWN, HID)
    dw = sum(dot(inputs[t], grad_rows[t]) for t in range(n_tiles))
    dw_out[...] = dw.reshape(n_y, 16, HID).astype(BF16)
    for i, feat in enumerate(column_sources):
        remote(9, dw_out.at[i], dw_in.at[i], g, feat).start()
    dw_in[n_y - 1] = dw_out[n_y - 1]

    wait_in(10, gz_in.at[pl.ds(0, n_graph - 1)])
    gfin[sheet] = jnp.sum(gz_in[...], axis=0).astype(BF16)
    for _, graph, feat in sheet_peers:
        remote(11, gfin.at[sheet], gfin.at[sheet], graph, feat).start()

    wait_in(9, dw_in.at[pl.ds(0, n_y - 1)])
    dz[...] = jnp.sum(dw_in[...].astype(F32), axis=0).astype(BF16)
    for peer in graphs:
        remote(12, dz, dz_in.at[g], peer, f).start()
    dz_in[g] = dz[...]

    hh_in[g] = jnp.zeros((2 * HALO, HID // 2), BF16)
    wait_in(7, hh_in.at[pl.ds(0, n_graph - 1)])
    halo = unfold(hh_in[...].astype(F32)).reshape(n_graph * HALO, HID)
    ext = jnp.concatenate([hidden.astype(F32), halo], axis=0).astype(BF16)
    mean2 = (dot_lhs_t(counts_t, ext) / FAN2).astype(BF16)
    out_ref[...] = (dot(hidden, w2_ref[0]) + dot(mean2, w2_ref[1])).astype(BF16)

    def unpack(ref, which):
        both = ref[...].astype(F32)
        g2_ref[which, :, 0:128] = both[:, :shard].reshape(HID, 128)
        g2_ref[which, :, 128:256] = both[:, shard:].reshape(HID, 128)

    wait_in(11, gfin.at[pl.ds(0, n_chip - 1)])
    remote(13, gfin, gsib, g, sibling).start()
    unpack(gfin, core)
    wait_in(12, dz_in.at[pl.ds(0, n_graph - 1)])
    g1_ref[...] = jnp.sum(dz_in[...].astype(F32), axis=0).reshape(2, 8, HID)
    wait_out(0, w_all.at[pl.ds(0, n_y - 1)])
    for t in range(n_tiles):
        wait_out(14 + t, x_all.at[t, pl.ds(0, n_y - 1)])
    wait_out(2, e_in.at[pl.ds(0, n_graph - 1)])
    wait_out(3, v_in)
    wait_out(4, pre_in.at[pl.ds(0, n_block - 1)])
    wait_out(5, hid_in)
    wait_out(6, d_all.at[pl.ds(0, n_block - 1)])
    wait_out(7, hh_in.at[pl.ds(0, n_graph - 1)])
    wait_out(8, gs_in.at[pl.ds(0, n_chip - 1)])
    wait_out(9, dw_in.at[pl.ds(0, n_y - 1)])
    wait_out(10, gz_in.at[pl.ds(0, n_graph - 1)])
    wait_out(11, gfin.at[pl.ds(0, n_chip - 1)])
    wait_out(12, dz_in.at[pl.ds(0, n_graph - 1)])
    wait_in(13, gsib)
    unpack(gsib, 1 - core)

    wait_out(13, gsib)


def store_kernel(a_ref, b_ref, c_ref, a_out, b_out, c_out, sem):
    copies = [
        pltpu.make_async_copy(src, dst, sem.at[i])
        for i, (src, dst) in enumerate(((b_ref, b_out), (a_ref, a_out), (c_ref, c_out)))
    ]
    for copy in copies:
        copy.start()
    for copy in copies:
        copy.wait()


def solution(mesh):
    n_graph, n_feat = mesh.shape["graph"], mesh.shape["feat"]
    n_chip, n_block = n_feat // 2, 2 * N_X
    n_y, n_tiles = n_chip // N_X, min(2, N_X)
    pack = 2 * HID // n_chip

    def body(features, w_first, w_second, cotangent, nbr_first, send_rows, nbr_second):
        vmem = pl.BlockSpec(memory_space=pltpu.VMEM)
        hbm = pl.BlockSpec(memory_space=pltpu.HBM)
        shapes = (
            jax.ShapeDtypeStruct((OWN, HID), BF16),
            jax.ShapeDtypeStruct((2, HID, HID), F32),
            jax.ShapeDtypeStruct((2, 8, HID), F32),
        )
        results = pl.pallas_call(
            functools.partial(kernel, n_graph, n_feat),
            out_shape=tuple(pltpu.VMEM(a.shape, a.dtype) for a in shapes),
            in_specs=[hbm] * 7,
            out_specs=(vmem,) * 3,
            scratch_shapes=[
                pltpu.VMEM((8, SRC), BF16),
                pltpu.VMEM((FAN1, n_feat * OWN), jnp.int32),
                pltpu.VMEM((2, HID, HID), BF16),
                pltpu.VMEM((OWN, HID), BF16),
                pltpu.VMEM((n_graph, HALO), jnp.int32),
                pltpu.VMEM((FAN2, OWN), jnp.int32),
                pltpu.VMEM((GROUPS * 8, LO), F32),
                pltpu.VMEM((n_tiles, n_y, 16, n_block // n_tiles * OWN), BF16),
                pltpu.VMEM((n_tiles, n_y, 16, n_block // n_tiles * OWN), BF16),
                pltpu.VMEM((n_y, 16, HID), BF16),
                pltpu.VMEM((n_block, OWN, HID), F32),
                pltpu.VMEM((n_block, OWN, HID), BF16),
                pltpu.VMEM((n_block, OWN, HID), BF16),
                pltpu.VMEM((n_block, OWN, HID), BF16),
                pltpu.VMEM((OWN, HID), BF16),
                pltpu.VMEM((OWN, HID), BF16),
                pltpu.VMEM((OWN, HID), BF16),
                pltpu.VMEM((OWN, HID), BF16),
                pltpu.VMEM((n_graph, 2 * HALO, HID // 2), BF16),
                pltpu.VMEM((n_graph, 2 * HALO, HID // 2), BF16),
                pltpu.VMEM((n_graph, 2 * HALO, HID // 2), BF16),
                pltpu.VMEM((n_graph, 2 * HALO, HID // 2), BF16),
                pltpu.VMEM((n_chip, pack, 128), BF16),
                pltpu.VMEM((n_chip, pack, 128), BF16),
                pltpu.VMEM((pack, 128), F32),
                pltpu.VMEM((n_graph, pack, 128), F32),
                pltpu.VMEM((n_chip, pack, 128), BF16),
                pltpu.VMEM((n_chip, pack, 128), BF16),
                pltpu.VMEM((n_y, 16, HID), BF16),
                pltpu.VMEM((n_y, 16, HID), BF16),
                pltpu.VMEM((16, HID), BF16),
                pltpu.VMEM((n_graph, 16, HID), BF16),
                pltpu.SemaphoreType.DMA((16,)),
                pltpu.SemaphoreType.DMA((16,)),
                pltpu.SemaphoreType.DMA((7,)),
            ],
            compiler_params=pltpu.CompilerParams(
                collective_id=0, has_side_effects=True, vmem_limit_bytes=40 * 1024 * 1024
            ),
        )(
            *(
                pltpu.with_memory_space_constraint(a, pltpu.HBM)
                for a in (
                    features.T,
                    w_first.reshape(16, HID),
                    w_second,
                    cotangent,
                    nbr_first.T,
                    send_rows.reshape(n_graph, HALO),
                    nbr_second.T,
                )
            )
        )
        return pl.pallas_call(
            store_kernel,
            out_shape=shapes,
            in_specs=[vmem] * 3,
            out_specs=(hbm,) * 3,
            scratch_shapes=[pltpu.SemaphoreType.DMA((3,))],
        )(*(pltpu.with_memory_space_constraint(a, pltpu.VMEM) for a in results))

    in_specs = (
        P("graph", "feat"),
        P(None, "feat", None),
        P(),
        P(("graph", "feat"), None),
        P("graph", None),
        P(("graph", "feat"), None, None),
        P(("graph", "feat"), None),
    )
    out_specs = (P(("graph", "feat"), None), P(), P(None, "feat", None))
    return jax.shard_map(body, mesh=mesh, in_specs=in_specs, out_specs=out_specs, check_vma=False)
```
